512 devices in a mesh: lat: 32 (over y, z_lo), lon: 16 (over x, z_hi, core).
Axes of the slice: x: 4, y: 8, z: 8 (z_hi: 2, z_lo: 4; z = z_hi * 4 + z_lo), core: 2. Of those that a mesh axis runs over, the one named last changes fastest.
Arguments:
- state_field: bfloat16 [384, 1024, 384], P('lat', 'lon'), may hold values from -6 to 6
- mix_weight: bfloat16 [384, 384, 384], P('lat', 'lon'), may hold values from -0.3125 to 0.3125
- upsample_weight: bfloat16 [384, 1024], replicated, may hold values from -0.3125 to 0.3125
- upsample_bias: float32 [64], replicated, may hold values from -3 to 3
- conv_weight: bfloat16 [9, 64, 64], replicated, may hold values from -0.25 to 0.25
- conv_bias: float32 [64], replicated, may hold values from -3 to 3
Outputs:
- fine_field: bfloat16 [64, 1536, 4096], P(None, 'lat', 'lon')
The draws below stay inside these ranges and needn't reach their ends.
All inputs are finite; a program needn't handle non-finite values.
Results may differ from the reference program's by a relative error of at most 0.012.
Values may be sent and summed in bfloat16 or wider, within the bound.
No kernel may reach another device: no remote copies, remote signals or barrier semaphores. Data moves between devices by JAX's collectives and lax.ppermute only.
A program may use at most 128 MiB of HBM per device.

```python
import math
import jax
import jax.numpy as jnp
from jax import lax

C = 384
FC = 64
NLAT = 384
NLON = 1024


def levels(key, dims, cuts, smallest, largest):
    def one(dim, shards_of):
        heights = jax.random.uniform(jax.random.fold_in(jax.random.fold_in(key, 6), dim), (shards_of,), jnp.float32, smallest / len(cuts), largest / len(cuts))
        return jnp.repeat(jnp.exp(heights), dims[dim] // shards_of).reshape((-1,) + (1,) * (len(dims) - dim - 1))

    factor_of = one(*cuts[0])
    for cut in cuts[1:]:
        factor_of = factor_of * one(*cut)
    return factor_of


def normal_values(rng, dims, spread, most, cuts=(), held_as=jnp.bfloat16):
    array = jax.random.normal(rng, dims, jnp.float32) * spread
    if len(cuts) > 0:
        array = levels(rng, dims, cuts, -0.22, 0.18) * array
    return jnp.clip(array, min=-most, max=most).astype(held_as)


def setup_inputs(seed: int = 0) -> dict:
    seeds = jax.random.split(jax.random.key(seed), 7)
    return {
        "state_field": normal_values(seeds[0], (NLAT, NLON, C), 1.0, 6.0, ((0, 32), (1, 16))),
        "mix_weight": normal_values(seeds[1], (NLAT, C, C), C ** -0.5, 0.3125, ((0, 32), (1, 16))),
        "upsample_weight": normal_values(seeds[2], (C, 16 * FC), C ** -0.5, 0.3125),
        "upsample_bias": normal_values(seeds[3], (FC,), 0.5, 3.0, (), jnp.float32),
        "conv_weight": normal_values(seeds[4], (9, FC, FC), (9 * FC) ** -0.5, 0.25),
        "conv_bias": normal_values(seeds[5], (FC,), 0.5, 3.0, (), jnp.float32),
    }


degree_block = 16

def start_logs(degrees):
    values = []
    running_total = 0.0
    for order_value in range(degrees):
        if order_value > 0:
            running_total = running_total + math.log((2.0 * order_value - 1.0) / (2.0 * order_value))
        values.append(0.5 * (math.log((2.0 * order_value + 1.0) / (4.0 * math.pi)) + running_total))
    return values

def legendre_setup(orders, lat_count, degrees):
    order_float = orders.astype(jnp.float32)[:, None]
    colatitude = (jnp.arange(lat_count, dtype=jnp.float32) + 0.5) * (math.pi / lat_count)
    cosine = jnp.cos(colatitude)[None, :]
    log_sine = jnp.log(jnp.sin(colatitude))[None, :]
    log_table = jnp.asarray(start_logs(degrees), jnp.float32)
    selector = orders[:, None] == jnp.arange(degrees, dtype=jnp.int32)[None, :]
    log_base = lax.optimization_barrier(jnp.sum(jnp.where(selector, log_table[None, :], 0.0), axis=1))[:, None]
    log_start = log_base + order_float * log_sine
    diagonal_start = jnp.where(log_start > -80.0, jnp.exp(jnp.maximum(log_start, -80.0)), 0.0)
    return (order_float, cosine, diagonal_start)

def legendre_block(loop_carry_state, first_degree, order_float, cosine, diagonal_start):
    previous, earlier = loop_carry_state
    row_list = []
    for step_index in range(degree_block):
        degree = (first_degree + step_index).astype(jnp.float32)
        above_diag = degree > order_float
        spacing = jnp.where(above_diag, degree * degree - order_float * order_float, 1.0)
        alpha_coef = jnp.where(above_diag, jnp.sqrt(jnp.maximum(4.0 * degree * degree - 1.0, 1.0) / spacing), 0.0)
        past_next = degree > order_float + 1.0
        previous_degree = degree - 1.0
        numerator = jnp.maximum(previous_degree * previous_degree - order_float * order_float, 0.0)
        beta_coef = jnp.where(past_next, jnp.sqrt(numerator / jnp.maximum(4.0 * previous_degree * previous_degree - 1.0, 1.0)), 0.0)
        current = alpha_coef * (cosine * previous - beta_coef * earlier) + jnp.where(degree == order_float, diagonal_start, 0.0)
        row_list.append(current)
        earlier = previous
        previous = current
    return ((previous, earlier), jnp.stack(row_list))

def quadrature(lat_count):
    colatitude = (jnp.arange(lat_count, dtype=jnp.float32) + 0.5) * (math.pi / lat_count)
    return jnp.sin(colatitude) * (math.pi / lat_count)

def analysis(spectra, orders, lat_count, degrees):
    order_float, cosine, diagonal_start = legendre_setup(orders, lat_count, degrees)
    zeros_grid = jnp.zeros((orders.shape[0], lat_count), jnp.float32)
    weights = quadrature(lat_count)[None, None, :]
    spectra_full_width = spectra.astype(jnp.float32)

    def advance(loop_carry_state, first_degree):
        loop_carry_state, basis = legendre_block(loop_carry_state, first_degree, order_float, cosine, diagonal_start)
        quadrature_weighted_basis = (weights * basis).astype(jnp.bfloat16).astype(jnp.float32)
        return (loop_carry_state, jnp.einsum('wxy,jyx->wjy', spectra_full_width, quadrature_weighted_basis, precision=lax.Precision.HIGHEST))
    firsts = jnp.arange(0, degrees, degree_block, dtype=jnp.int32)
    _, stacked = lax.scan(advance, (zeros_grid, zeros_grid), firsts)
    return jnp.transpose(stacked, (1, 0, 2, 3)).reshape(spectra.shape[0], degrees, orders.shape[0])

def synthesis(coeff_values, orders, lat_count, degrees):
    order_float, cosine, diagonal_start = legendre_setup(orders, lat_count, degrees)
    channels = coeff_values.shape[0]
    zeros_grid = jnp.zeros((orders.shape[0], lat_count), jnp.float32)
    blocks = jnp.transpose(coeff_values.astype(jnp.float32).reshape(channels, degrees // degree_block, degree_block, orders.shape[0]), (1, 0, 2, 3))

    def advance(loop_carry_state, inputs):
        first_degree, coefficient_slice = inputs
        previous, earlier, running_total = loop_carry_state
        (previous, earlier), basis = legendre_block((previous, earlier), first_degree, order_float, cosine, diagonal_start)
        unweighted_basis = basis.astype(jnp.bfloat16).astype(jnp.float32)
        running_total = running_total + jnp.einsum('smi,mih->shi', coefficient_slice, unweighted_basis, precision=lax.Precision.HIGHEST)
        return ((previous, earlier, running_total), None)
    firsts = jnp.arange(0, degrees, degree_block, dtype=jnp.int32)
    start_carry = (zeros_grid, zeros_grid, jnp.zeros((channels, lat_count, orders.shape[0]), jnp.float32))
    final_carry, _ = lax.scan(advance, start_carry, (firsts, blocks))
    return final_carry[2]

def fourier_tables(lon_count, wave_count):
    longitude = jnp.arange(lon_count, dtype=jnp.int32)
    wave_index = jnp.arange(wave_count, dtype=jnp.int32)
    phase_index = longitude[:, None] * wave_index[None, :] % lon_count
    angles = phase_index.astype(jnp.float32) * (2.0 * math.pi / lon_count)
    step_scale = 2.0 * math.pi / lon_count
    forward = jnp.concatenate([jnp.cos(angles) * step_scale, -jnp.sin(angles) * step_scale], axis=1).astype(jnp.bfloat16)
    doubling = jnp.where(wave_index == 0, 1.0, 2.0).astype(jnp.float32)[:, None]
    inverse = jnp.concatenate([jnp.cos(angles).T * doubling, -jnp.sin(angles).T * doubling], axis=0).astype(jnp.bfloat16)
    return (forward, inverse)

def upsample(hidden, upsample_weight, upsample_bias):
    channels, row_count, col_count = hidden.shape
    fine_channels = upsample_bias.shape[0]
    projected = lax.dot_general(upsample_weight, hidden.reshape(channels, row_count * col_count), (((0,), (0,)), ((), ())), preferred_element_type=jnp.float32)
    projected = projected.reshape(fine_channels, 4, 4, row_count, col_count) + upsample_bias.astype(jnp.float32)[:, None, None, None, None]
    fine_grid = jax.nn.gelu(projected).astype(jnp.bfloat16)
    return jnp.transpose(fine_grid, (0, 3, 1, 4, 2)).reshape(fine_channels, 4 * row_count, 4 * col_count)

def convolve(framed, conv_weight, conv_bias, fine_grid):
    fine_channels, row_count, col_count = fine_grid.shape
    accumulated = jnp.zeros((fine_channels, row_count * col_count), jnp.float32)
    for tap_index in range(9):
        tap_row = tap_index // 3
        tap_col = tap_index % 3
        shifted = framed[:, tap_row:tap_row + row_count, tap_col:tap_col + col_count].reshape(fine_channels, row_count * col_count)
        accumulated = accumulated + jnp.dot(conv_weight[tap_index], shifted, preferred_element_type=jnp.float32)
    total = fine_grid.astype(jnp.float32) + accumulated.reshape(fine_channels, row_count, col_count) + conv_bias.astype(jnp.float32)[:, None, None]
    return total.astype(jnp.bfloat16)

def reference(state_field, mix_weight, upsample_weight, upsample_bias, conv_weight, conv_bias):
    state_first = jnp.transpose(state_field, (2, 0, 1))
    forward, inverse = fourier_tables(NLON, NLAT)
    spectra = jnp.dot(state_first.reshape(C * NLAT, NLON), forward, preferred_element_type=jnp.float32)
    spectra = spectra.astype(jnp.bfloat16).reshape(C, NLAT, 2 * NLAT)
    orders = jnp.arange(2 * NLAT, dtype=jnp.int32) % NLAT
    coeffs = analysis(spectra, orders, NLAT, NLAT).astype(jnp.bfloat16)
    mixed_modes = jnp.einsum('loi,ilk->olk', mix_weight.astype(jnp.float32), coeffs.astype(jnp.float32), precision=lax.Precision.HIGHEST).astype(jnp.bfloat16)
    synthesized = synthesis(mixed_modes, orders, NLAT, NLAT).astype(jnp.bfloat16)
    spatial = jnp.dot(synthesized.reshape(C * NLAT, 2 * NLAT), inverse, preferred_element_type=jnp.float32).reshape(C, NLAT, NLON)
    hidden = (state_first.astype(jnp.float32) + jax.nn.gelu(spatial)).astype(jnp.bfloat16)
    fine_grid = upsample(hidden, upsample_weight, upsample_bias)
    framed = jnp.pad(fine_grid, ((0, 0), (0, 0), (1, 1)), mode='wrap')
    framed = jnp.pad(framed, ((0, 0), (1, 1), (0, 0)))
    return convolve(framed, conv_weight, conv_bias, fine_grid)
```

```python
import math

import jax
import jax.numpy as jnp
from jax import lax
from jax.experimental import pallas as pl
from jax.experimental.pallas import tpu as pltpu
from jax.sharding import Mesh
from jax.sharding import PartitionSpec as P

f32 = jnp.float32
bf16 = jnp.bfloat16
MIB = 1 << 20


def call(kernel, out, *args, scratch=(), flops=0, smem=(), vmem=40):
    space = [
        pl.BlockSpec(memory_space=pltpu.SMEM if i in smem else pltpu.VMEM) for i in range(len(args))
    ]
    outs = out if isinstance(out, (tuple, list)) else (out,)
    moved = sum(x.size * x.dtype.itemsize for x in (*args, *outs))
    return pl.pallas_call(
        kernel,
        out_shape=out,
        in_specs=space,
        out_specs=jax.tree.map(lambda _: pl.BlockSpec(memory_space=pltpu.VMEM), out),
        scratch_shapes=list(scratch),
        compiler_params=pltpu.CompilerParams(vmem_limit_bytes=vmem * MIB),
        cost_estimate=pl.CostEstimate(flops=flops, bytes_accessed=moved, transcendentals=0),
    )(*args)


def shape(dims, dtype=bf16):
    return jax.ShapeDtypeStruct(dims, dtype)


def iota(dims, axis):
    return lax.broadcasted_iota(jnp.int32, dims, axis)


def widen():
    row, col = iota((384, 512), 0), iota((384, 512), 1)
    return jnp.where((col % 128 < 96) & (row == col // 128 * 96 + col % 128), 1.0, 0.0).astype(bf16)


def dot(a, b):
    return jnp.dot(a, b, preferred_element_type=f32)


def dot_nt(a, b):
    return lax.dot_general(a, b, (((1,), (1,)), ((), ())), preferred_element_type=f32)


def pack_kernel(x_ref, s_ref):
    spread = widen()
    for a in range(12):
        wide = dot(x_ref[a], spread).astype(bf16)
        for b in range(4):
            s_ref[
                pl.ds((a // 3 * 4 + b) * 64, 64), pl.ds(a % 3 * 128, 128)
            ] = wide[:, b * 128 : (b + 1) * 128]


def dft_tables_kernel(p_ref, q_ref, cb_ref, sb_ref, pt_ref, qt_ref, cbt_ref, sbt_ref, c_ref, g_ref):
    for b in range(8):
        c_ref[:, pl.ds(b * 128, 128)] = (
            p_ref[...] * cb_ref[:, b : b + 1] - q_ref[...] * sb_ref[:, b : b + 1]
        ).astype(bf16)
        g_ref[pl.ds(b * 128, 128), :] = (
            pt_ref[...] * cbt_ref[b : b + 1, :] - qt_ref[...] * sbt_ref[b : b + 1, :]
        ).astype(bf16)


def dft_kernel(c_ref, x_ref, w_ref, s_ref):
    for block in range(4):
        rows = pl.ds(block * 256, 256)
        s_ref[rows, :] = (dot(c_ref[rows, :], x_ref[...]) * w_ref[...]).astype(bf16)


def legendre_tables_kernel(order_ref, cosine_ref, start_ref, l_ref, t_ref, rows_ref):
    order = order_ref[...]
    squared = order * order
    rows_ref[...] = jnp.zeros(rows_ref.shape, f32)

    def step(l, carry):
        previous, earlier = carry
        degree = l.astype(f32)
        above = degree > order
        spacing = jnp.where(above, degree * degree - squared, 1.0)
        alpha = jnp.where(
            above, jnp.sqrt(jnp.maximum(4.0 * degree * degree - 1.0, 1.0) / spacing), 0.0
        )
        below = degree - 1.0
        beta = jnp.where(
            degree > order + 1.0,
            jnp.sqrt(
                jnp.maximum(below * below - squared, 0.0)
                / jnp.maximum(4.0 * below * below - 1.0, 1.0)
            ),
            0.0,
        )
        first = degree == order
        current = []
        for t in range(3):
            lanes = pl.ds(t * 128, 128)
            value = alpha * (cosine_ref[:, lanes] * previous[t] - beta * earlier[t]) + jnp.where(
                first, start_ref[:, lanes], 0.0
            )
            rows_ref[t, pl.ds(pl.multiple_of(l * 8, 8), 8), :] = value
            current.append(value)
        return (tuple(current), previous)

    zeros = (jnp.zeros((8, 128), f32),) * 3

    def block(i, carry):
        for u in range(8):
            carry = step(i * 8 + u, carry)
        return carry

    lax.fori_loop(0, 48, block, (zeros, zeros))
    for m3 in range(3):
        for t in range(3):
            parts = [rows_ref[t, pl.ds(r * 8 + m3, 128, stride=24), :] for r in range(3)]
            table = jnp.concatenate(parts, axis=0)
            l_ref[m3, :, pl.ds(t * 128, 128)] = table.astype(bf16)
            t_ref[m3, pl.ds(t * 128, 128), :] = table.T.astype(bf16)


def legendre_kernel(x_ref, l_ref, s_ref, in_ref, out_ref):
    for t in range(3):
        in_ref[t] = x_ref[:, t * 128 : (t + 1) * 128].astype(f32)
    out_ref[...] = jnp.zeros(out_ref.shape, f32)
    for m3 in range(3):
        halves = [
            jnp.concatenate(
                [in_ref[t, pl.ds(cs * 3 + m3, 128, stride=8), :] for t in range(3)], axis=0
            )
            for cs in range(2)
        ]
        result = dot(l_ref[m3], jnp.concatenate(halves, axis=1).astype(bf16))
        for t in range(3):
            for cs in range(2):
                out_ref[t, pl.ds(cs * 3 + m3, 128, stride=8), :] = result[
                    t * 128 : (t + 1) * 128, cs * 128 : (cs + 1) * 128
                ]
    for t in range(3):
        s_ref[:, pl.ds(t * 128, 128)] = out_ref[t].astype(bf16)


def mix_weight_kernel(first_ref, w_ref, o_ref):
    del first_ref
    part = w_ref[...].astype(f32).reshape(384, 384).astype(bf16)
    wide = dot(part, widen()).astype(bf16)
    o_ref[...] = jnp.zeros(o_ref.shape, bf16)
    for b in range(4):
        o_ref[0, pl.ds(b * 128, 96), :] = wide[b * 96 : (b + 1) * 96]


def spread_mix_weight(gathered, first):
    return pl.pallas_call(
        mix_weight_kernel,
        out_shape=shape((3, 512, 512)),
        grid_spec=pltpu.PrefetchScalarGridSpec(
            num_scalar_prefetch=1,
            grid=(3,),
            in_specs=[pl.BlockSpec((16, 1, 24, 384), lambda r, first: (0, first[0] + r, 0, 0))],
            out_specs=pl.BlockSpec((1, 512, 512), lambda r, first: (r, 0, 0)),
        ),
        compiler_params=pltpu.CompilerParams(vmem_limit_bytes=24 * MIB),
        cost_estimate=pl.CostEstimate(flops=10**9, bytes_accessed=3 * 10**6, transcendentals=0),
    )(first, gathered)


def mix_kernel(x_ref, w_ref, s_ref):
    for r in range(3):
        lanes = pl.ds(r * 128, 128)
        part = x_ref[:, lanes].astype(f32).reshape(32, 4, 8, 128)
        modes = jnp.concatenate([part[:, b].reshape(256, 128) for b in range(4)], axis=1)
        mixed = dot_nt(modes.astype(bf16), w_ref[r])
        back = [mixed[:, b * 128 : (b + 1) * 128].reshape(32, 1, 8, 128) for b in range(4)]
        s_ref[:, lanes] = jnp.concatenate(back, axis=1).reshape(1024, 128).astype(bf16)


def inverse_kernel(g_ref, x_ref, state_ref, s_ref, h_ref):
    for block in range(4):
        rows = pl.ds(block * 256, 256)
        spatial = dot(g_ref[rows, :], x_ref[...])
        hidden = (state_ref[rows, :].astype(f32) + jax.nn.gelu(spatial)).astype(bf16)
        h_ref[rows, :] = hidden.astype(f32)
        for part in range(4):
            s_ref[pl.ds((block * 4 + part) * 80, 64), :] = hidden[part * 64 : (part + 1) * 64]
    row = iota((16, 384), 0)
    for q in range(16):
        right = h_ref[pl.ds((q + 1) % 16 * 64, 1), :]
        left = h_ref[pl.ds((q * 64 + 1023) % 1024, 1), :]
        edge = jnp.where(row == 0, right, jnp.where(row == 15, left, 0.0))
        s_ref[pl.ds(q * 80 + 64, 16), :] = edge.astype(bf16)


def tail_weights_kernel(u_ref, w_ref, o_ref, c_ref):
    o_ref[...] = jnp.zeros(o_ref.shape, bf16)
    row, col = iota((1024, 256), 0), iota((1024, 256), 1)
    for q in range(4):
        pick = jnp.where(row == 16 * (col % 64) + 4 * (col // 64) + q, 1.0, 0.0).astype(bf16)
        part = dot(u_ref[...], pick).astype(bf16)
        for b in range(4):
            o_ref[pl.ds(b * 128, 96), pl.ds(q * 256, 256)] = part[b * 96 : (b + 1) * 96]
    for ds in range(3):
        for p in range(4):
            blocks = []
            for window in (0, 1, 2, 3, 4, -1):
                dr = window - p
                if -1 <= dr <= 1:
                    blocks.append(w_ref[3 * (dr + 1) + ds].astype(f32))
                else:
                    blocks.append(jnp.zeros((64, 64), f32))
            c_ref[ds, pl.ds(p * 64, 64), :] = jnp.concatenate(blocks, axis=1).astype(bf16)


def fine_kernel(x_ref, u_ref, bias_ref, o_ref, h_ref):
    for a in range(12):
        for b in range(4):
            h_ref[pl.ds(a * 80, 80), pl.ds(b * 128, 128)] = x_ref[
                pl.ds((a // 3 * 4 + b) * 80, 80), pl.ds(a % 3 * 128, 128)
            ]
    for q in range(4):
        lanes = pl.ds(q * 256, 256)
        for block in range(4):
            rows = pl.ds(block * 240, 240)
            value = dot(h_ref[rows, :], u_ref[:, lanes]) + bias_ref[:, lanes]
            o_ref[q, rows, :] = jax.nn.gelu(value).astype(bf16)


def conv_kernel(
    ends_ref, f_ref, up_ref, down_ref, u_ref, bias_ref, w_ref, cb_ref, o_ref,
    h_ref, e_ref, t_ref, s_ref, z_ref, g_ref,
):
    for b in range(4):
        lanes = pl.ds(b * 128, 128)
        h_ref[pl.ds(0, 80), lanes] = up_ref[pl.ds(b * 80, 80), :]
        h_ref[pl.ds(80, 80), lanes] = down_ref[pl.ds(b * 80, 80), :]
    first = iota((160, 256), 0) < 80
    keep = jnp.where(first, ends_ref[0], ends_ref[1]) > 0
    half = iota((80, 128), 1) < 64
    for q in range(4):
        lanes = pl.ds(q * 256, 256)
        value = jax.nn.gelu(dot(h_ref[...], u_ref[:, lanes]) + bias_ref[:, lanes])
        e_ref[...] = jnp.where(keep, value, 0.0).astype(bf16)
        for a in range(12):
            below = e_ref[pl.ds(80, 80), 0:128] if a == 11 else f_ref[q, pl.ds(a * 80 + 80, 80), 0:128]
            above = e_ref[pl.ds(0, 80), 128:256] if a == 0 else f_ref[q, pl.ds(a * 80 - 80, 80), 128:256]
            t_ref[q, pl.ds(a * 80, 80), :] = jnp.where(half, below, above)
    for side, q, amount in ((0, 3, 1), (1, 0, 79)):
        for a in range(12):
            rows = pl.ds(a * 80, 80)
            for t in range(3):
                part = t_ref[q, rows, :] if t == 2 else f_ref[q, rows, t * 128 : (t + 1) * 128]
                s_ref[side, rows, pl.ds(t * 128, 128)] = pltpu.roll(
                    part.astype(f32), amount, 0
                ).astype(bf16)
    for q in range(4):
        total = f_ref[q].astype(f32) + cb_ref[...]
        for ds in range(3):
            source = q + ds - 1
            if 0 <= source < 4:
                total = total + dot_nt(f_ref[source], w_ref[ds, :, 0:256])
                total = total + dot_nt(t_ref[source], w_ref[ds, :, 256:384])
            else:
                total = total + dot_nt(s_ref[0 if source < 0 else 1], w_ref[ds])
        z_ref[q] = total.astype(bf16)
    row, col = iota((256, 256), 0), iota((256, 256), 1)
    place = jnp.where(col == 4 * (row % 64) + row // 64, 1.0, 0.0).astype(bf16)
    for a in range(12):
        cells = jnp.concatenate([z_ref[q, pl.ds(a * 80, 64), :] for q in range(4)], axis=0)
        lines = lax.dot_general(cells, place, (((0,), (0,)), ((), ())), preferred_element_type=f32)
        for p in range(4):
            for t in range(2):
                g_ref[t, pl.ds(4 * a + p, 64, stride=48), :] = lines[
                    p * 64 : (p + 1) * 64, t * 128 : (t + 1) * 128
                ]
    for t in range(2):
        o_ref[:, :, pl.ds(t * 128, 128)] = g_ref[t].reshape(64, 48, 128).astype(bf16)


def start_logs(degrees):
    values = []
    total = 0.0
    for m in range(degrees):
        if m > 0:
            total = total + math.log((2.0 * m - 1.0) / (2.0 * m))
        values.append(0.5 * (math.log((2.0 * m + 1.0) / (4.0 * math.pi)) + total))
    return values


def legendre_tables(n):
    order = 3 * n + jnp.arange(8, dtype=jnp.int32)
    lane = jnp.arange(384, dtype=jnp.int32)
    colatitude = ((3 * (lane % 128) + lane // 128).astype(f32) + 0.5) * (math.pi / 384)
    cosine = jnp.broadcast_to(jnp.cos(colatitude)[None, :], (8, 384))
    log_sine = jnp.log(jnp.sin(colatitude))[None, :]
    logs = jnp.asarray(start_logs(384), f32)
    log_base = jnp.sum(jnp.where(order[:, None] == lane[None, :], logs[None, :], 0.0), axis=1)
    log_start = log_base[:, None] + order.astype(f32)[:, None] * log_sine
    start = jnp.where(log_start > -80.0, jnp.exp(jnp.maximum(log_start, -80.0)), 0.0)
    orders = jnp.broadcast_to(order.astype(f32)[:, None], (8, 128))
    return call(
        legendre_tables_kernel,
        (shape((3, 384, 384)), shape((3, 384, 384))),
        orders,
        cosine,
        start,
        scratch=[pltpu.VMEM((3, 3072, 128), f32)],
        flops=4 * 10**9,
    )


def dft_tables():
    step = 2.0 * math.pi / 1024

    def base(row_axis, dims):
        k, y = iota(dims, row_axis), iota(dims, 1 - row_axis)
        j = k % 8
        wave = 3 * (k // 8) + j % 3
        used = j < 6
        angle = ((wave * y + jnp.where(j < 3, 0, 256)) % 1024).astype(f32) * step
        scale = jnp.where(used, 1.0, 0.0)
        if row_axis == 1:
            scale = scale * jnp.where(wave == 0, 1.0, 2.0)
        turn = (wave * y % 8).astype(f32) * (math.pi / 4)
        return jnp.cos(angle) * scale, jnp.sin(angle) * scale, turn

    p, q, _ = base(0, (1024, 128))
    turn = base(0, (1024, 8))[2]
    pt, qt, _ = base(1, (128, 1024))
    turn_t = base(1, (8, 1024))[2]
    return call(
        dft_tables_kernel,
        (shape((1024, 1024)), shape((1024, 1024))),
        p, q, jnp.cos(turn), jnp.sin(turn), pt, qt, jnp.cos(turn_t), jnp.sin(turn_t),
        flops=4 * 10**9,
    )


def exchange(x, axes):
    return lax.all_to_all(x, axes, 0, 0, tiled=True)


def local(state_field, mix_weight, upsample_weight, upsample_bias, conv_weight, conv_bias):
    lat, qa, qb = lax.axis_index("lat"), lax.axis_index("qa"), lax.axis_index("qb")
    n = 4 * lat + qa
    gathered = lax.all_gather(mix_weight, ("qa", "qb"), axis=0)
    packed = call(pack_kernel, shape((1024, 384)), state_field, flops=10**9)
    state = exchange(packed, ("qa", "qb"))
    forward, inverse = dft_tables()
    colatitude = ((3 * n + jnp.arange(384, dtype=jnp.int32) // 128).astype(f32) + 0.5) * (
        math.pi / 384
    )
    scale = (jnp.sin(colatitude) * (math.pi / 384) * (2.0 * math.pi / 1024))[None, :]
    spectra = call(dft_kernel, shape((1024, 384)), forward, state, scale, flops=10**9)
    columns = exchange(spectra, ("lat", "qa"))
    basis, basis_t = legendre_tables(n)
    scratch = [pltpu.VMEM((3, 1024, 128), f32)] * 2
    coeffs = call(legendre_kernel, shape((1024, 384)), columns, basis, scratch=scratch, flops=10**9)
    degrees = exchange(coeffs, ("lat", "qb"))
    mixer = spread_mix_weight(gathered, (3 * qb).reshape(1).astype(jnp.int32))
    mixed = call(mix_kernel, shape((1024, 384)), degrees, mixer, flops=10**9)
    returned = exchange(mixed, ("lat", "qb"))
    synthesized = call(
        legendre_kernel, shape((1024, 384)), returned, basis_t, scratch=scratch, flops=10**9
    )
    modes = exchange(synthesized, ("lat", "qa"))
    hidden = call(
        inverse_kernel,
        shape((1280, 384)),
        inverse,
        modes,
        state,
        scratch=[pltpu.VMEM((1024, 384), f32)],
        flops=10**9,
    )
    cells = exchange(hidden, ("qa", "qb"))
    spread_up, spread_conv = call(
        tail_weights_kernel,
        (shape((512, 1024)), shape((3, 256, 384))),
        upsample_weight,
        conv_weight,
        flops=2 * 10**9,
    )
    first_row = cells[0:320, 0:128]
    last_row = cells[960:1280, 256:384]
    count = lax.axis_size("lat")
    up = lax.ppermute(last_row, "lat", [(i, i + 1) for i in range(count - 1)])
    down = lax.ppermute(first_row, "lat", [(i + 1, i) for i in range(count - 1)])
    bias = jnp.tile(upsample_bias, 16)[None, :]
    fine = call(
        fine_kernel,
        shape((4, 960, 256)),
        cells,
        spread_up,
        bias,
        scratch=[pltpu.VMEM((960, 512), bf16)],
        flops=10**10,
    )
    ends = jnp.stack([lat > 0, lat < count - 1]).astype(jnp.int32)
    return call(
        conv_kernel,
        shape((64, 48, 256)),
        ends,
        fine,
        up,
        down,
        spread_up,
        bias,
        spread_conv,
        jnp.tile(conv_bias, 4)[None, :],
        smem=(0,),
        scratch=[
            pltpu.VMEM((160, 512), bf16),
            pltpu.VMEM((160, 256), bf16),
            pltpu.VMEM((4, 960, 128), bf16),
            pltpu.VMEM((2, 960, 384), bf16),
            pltpu.VMEM((4, 960, 256), bf16),
            pltpu.VMEM((2, 3072, 128), f32),
        ],
        flops=10**10,
    )


def solution(mesh):
    fine_mesh = Mesh(mesh.devices.reshape(32, 4, 4), ("lat", "qa", "qb"))
    rows = P("lat", ("qa", "qb"), None)
    return jax.shard_map(
        local,
        mesh=fine_mesh,
        in_specs=(rows, rows, P(), P(), P(), P()),
        out_specs=P(None, "lat", ("qa", "qb")),
        check_vma=False,
    )
```

```python
import math

import jax
import jax.numpy as jnp
from jax import lax
from jax.experimental import pallas as pl
from jax.experimental.pallas import tpu as pltpu
from jax.sharding import Mesh
from jax.sharding import PartitionSpec as P

f32 = jnp.float32
bf16 = jnp.bfloat16
MIB = 1 << 20


def call(kernel, out, *args, scratch=(), flops=0, smem=(), vmem=40):
    space = [
        pl.BlockSpec(memory_space=pltpu.SMEM if i in smem else pltpu.VMEM) for i in range(len(args))
    ]
    outs = out if isinstance(out, (tuple, list)) else (out,)
    moved = sum(x.size * x.dtype.itemsize for x in (*args, *outs))
    return pl.pallas_call(
        kernel,
        out_shape=out,
        in_specs=space,
        out_specs=jax.tree.map(lambda _: pl.BlockSpec(memory_space=pltpu.VMEM), out),
        scratch_shapes=list(scratch),
        compiler_params=pltpu.CompilerParams(vmem_limit_bytes=vmem * MIB),
        cost_estimate=pl.CostEstimate(flops=flops, bytes_accessed=moved, transcendentals=0),
    )(*args)


def shape(dims, dtype=bf16):
    return jax.ShapeDtypeStruct(dims, dtype)


def iota(dims, axis):
    return lax.broadcasted_iota(jnp.int32, dims, axis)


def widen():
    row, col = iota((384, 512), 0), iota((384, 512), 1)
    return jnp.where((col % 128 < 96) & (row == col // 128 * 96 + col % 128), 1.0, 0.0).astype(bf16)


def dot(a, b):
    return jnp.dot(a, b, preferred_element_type=f32)


def dot_nt(a, b):
    return lax.dot_general(a, b, (((1,), (1,)), ((), ())), preferred_element_type=f32)


def lanes_of(x):
    return iota(x.shape, 1)


def close(first, middle, last):
    lane = lanes_of(first)
    return (
        jnp.where(lane < 96, first, pltpu.roll(middle, 96, 1)),
        jnp.where(lane < 96, last, pltpu.roll(middle, 64, 1)),
    )


def reopen(first, last, rest):
    lane = lanes_of(first)
    return jnp.where(
        lane < 32, pltpu.roll(first, 32, 1), jnp.where(lane < 64, pltpu.roll(last, 64, 1), rest)
    )


def side_by_side(parts):
    group = lanes_of(parts[0]) // 32
    total = jnp.zeros(parts[0].shape, f32)
    for i, part in enumerate(parts):
        total = jnp.where(group == i, pltpu.roll(part, (32 * i + 64) % 128, 1), total)
    return total


def apart(x, i):
    return pltpu.roll(x, (64 - 32 * i) % 128, 1)


def close_cells(first, middle, last):
    a, b = close(first, middle, last)
    pieces = [middle[8 * g : 8 * g + 8] for g in range(8)]
    return (
        jnp.concatenate([a, side_by_side(pieces[:4])], axis=0),
        jnp.concatenate([b, side_by_side(pieces[4:])], axis=0),
    )


def reopen_cells(first, last):
    rest = [apart(first[64:72], i) for i in range(4)] + [apart(last[64:72], i) for i in range(4)]
    return reopen(first[:64], last[:64], jnp.concatenate(rest, axis=0))


def mode_row(j):
    return pl.ds(j, 128, stride=8)


def close_modes(y_ref, s_ref):
    a, b = close(y_ref[0], y_ref[1], y_ref[2])
    y_ref[0], y_ref[2] = a, b
    y_ref[0, mode_row(6), :] = side_by_side([y_ref[1, mode_row(j), :] for j in range(4)])
    y_ref[2, mode_row(6), :] = side_by_side([y_ref[1, mode_row(j), :] for j in range(4, 6)])
    s_ref[:, 0:128] = y_ref[0].astype(bf16)
    s_ref[:, 128:256] = y_ref[2].astype(bf16)


def reopen_modes(x_ref, y_ref):
    first, last = x_ref[:, 0:128].astype(f32), x_ref[:, 128:256].astype(f32)
    y_ref[0], y_ref[2] = first, last
    y_ref[1] = reopen(first, last, jnp.zeros(first.shape, f32))
    rest = y_ref[0, mode_row(6), :], y_ref[2, mode_row(6), :]
    upper = lanes_of(rest[0]) >= 64
    for j in range(6):
        y_ref[1, mode_row(j), :] = jnp.where(
            upper, apart(rest[j // 4], j % 4), y_ref[1, mode_row(j), :]
        )


def pack_kernel(x_ref, s_ref):
    spread = widen()
    for a in range(4):
        wide = [dot(x_ref[3 * a + t], spread) for t in range(3)]
        for b in range(4):
            first, last = close_cells(*(w[:, b * 128 : (b + 1) * 128] for w in wide))
            s_ref[a * 4 + b, :, 0:128] = first.astype(bf16)
            s_ref[a * 4 + b, :, 128:256] = last.astype(bf16)


def dft_tables_kernel(p_ref, q_ref, cb_ref, sb_ref, pt_ref, qt_ref, cbt_ref, sbt_ref, c_ref, g_ref):
    for b in range(8):
        c_ref[:, pl.ds(b * 128, 128)] = (
            p_ref[...] * cb_ref[:, b : b + 1] - q_ref[...] * sb_ref[:, b : b + 1]
        ).astype(bf16)
        g_ref[pl.ds(b * 128, 128), :] = (
            pt_ref[...] * cbt_ref[b : b + 1, :] - qt_ref[...] * sbt_ref[b : b + 1, :]
        ).astype(bf16)


def dft_kernel(c_ref, x_ref, w_ref, s_ref, state_ref, y_ref):
    for q in range(16):
        cells = x_ref[q].astype(f32)
        first, last = cells[:, 0:128], cells[:, 128:256]
        rows = pl.ds(q * 64, 64)
        state_ref[rows, 0:128] = first[:64].astype(bf16)
        state_ref[rows, 128:256] = reopen_cells(first, last).astype(bf16)
        state_ref[rows, 256:384] = last[:64].astype(bf16)
    for block in range(4):
        rows = pl.ds(block * 256, 256)
        result = dot(c_ref[rows, :], state_ref[...]) * w_ref[...]
        for t in range(3):
            y_ref[t, rows, :] = result[:, t * 128 : (t + 1) * 128]
    close_modes(y_ref, s_ref)


def legendre_tables_kernel(order_ref, cosine_ref, start_ref, l_ref, t_ref, rows_ref):
    order = order_ref[...]
    squared = order * order
    rows_ref[...] = jnp.zeros(rows_ref.shape, f32)

    def step(l, carry):
        previous, earlier = carry
        degree = l.astype(f32)
        above = degree > order
        spacing = jnp.where(above, degree * degree - squared, 1.0)
        alpha = jnp.where(
            above, jnp.sqrt(jnp.maximum(4.0 * degree * degree - 1.0, 1.0) / spacing), 0.0
        )
        below = degree - 1.0
        beta = jnp.where(
            degree > order + 1.0,
            jnp.sqrt(
                jnp.maximum(below * below - squared, 0.0)
                / jnp.maximum(4.0 * below * below - 1.0, 1.0)
            ),
            0.0,
        )
        first = degree == order
        current = []
        for t in range(3):
            lanes = pl.ds(t * 128, 128)
            value = alpha * (cosine_ref[:, lanes] * previous[t] - beta * earlier[t]) + jnp.where(
                first, start_ref[:, lanes], 0.0
            )
            rows_ref[t, pl.ds(pl.multiple_of(l * 8, 8), 8), :] = value
            current.append(value)
        return (tuple(current), previous)

    zeros = (jnp.zeros((8, 128), f32),) * 3

    def block(i, carry):
        for u in range(8):
            carry = step(i * 8 + u, carry)
        return carry

    lax.fori_loop(0, 48, block, (zeros, zeros))
    for m3 in range(3):
        for t in range(3):
            parts = [rows_ref[t, pl.ds(r * 8 + m3, 128, stride=24), :] for r in range(3)]
            table = jnp.concatenate(parts, axis=0)
            l_ref[m3, :, pl.ds(t * 128, 128)] = table.astype(bf16)
            t_ref[m3, pl.ds(t * 128, 128), :] = table.T.astype(bf16)


def legendre_kernel(x_ref, l_ref, s_ref, in_ref, out_ref):
    reopen_modes(x_ref, in_ref)
    out_ref[...] = jnp.zeros(out_ref.shape, f32)
    for m3 in range(3):
        halves = [
            jnp.concatenate(
                [in_ref[t, pl.ds(cs * 3 + m3, 128, stride=8), :] for t in range(3)], axis=0
            )
            for cs in range(2)
        ]
        result = dot(l_ref[m3], jnp.concatenate(halves, axis=1).astype(bf16))
        for t in range(3):
            for cs in range(2):
                out_ref[t, pl.ds(cs * 3 + m3, 128, stride=8), :] = result[
                    t * 128 : (t + 1) * 128, cs * 128 : (cs + 1) * 128
                ]
    close_modes(out_ref, s_ref)


def mix_weight_kernel(w_ref, o_ref):
    part = w_ref[...].astype(f32).reshape(384, 384).astype(bf16)
    wide = dot(part, widen()).astype(bf16)
    o_ref[...] = jnp.zeros(o_ref.shape, bf16)
    for b in range(4):
        o_ref[0, pl.ds(b * 128, 96), :] = wide[b * 96 : (b + 1) * 96]


def spread_mix_weight(gathered):
    return pl.pallas_call(
        mix_weight_kernel,
        out_shape=shape((3, 512, 512)),
        grid=(3,),
        in_specs=[pl.BlockSpec((16, 1, 24, 384), lambda r: (0, r, 0, 0))],
        out_specs=pl.BlockSpec((1, 512, 512), lambda r: (r, 0, 0)),
        compiler_params=pltpu.CompilerParams(vmem_limit_bytes=24 * MIB),
        cost_estimate=pl.CostEstimate(flops=10**9, bytes_accessed=3 * 10**6, transcendentals=0),
    )(gathered)


def mix_kernel(x_ref, w_ref, s_ref, in_ref, out_ref):
    reopen_modes(x_ref, in_ref)
    for r in range(3):
        part = in_ref[r].reshape(32, 4, 8, 128)
        modes = jnp.concatenate([part[:, b].reshape(256, 128) for b in range(4)], axis=1)
        mixed = dot_nt(modes.astype(bf16), w_ref[r])
        back = [mixed[:, b * 128 : (b + 1) * 128].reshape(32, 1, 8, 128) for b in range(4)]
        out_ref[r] = jnp.concatenate(back, axis=1).reshape(1024, 128)
    close_modes(out_ref, s_ref)


def inverse_kernel(g_ref, x_ref, state_ref, s_ref, y_ref, m_ref, h_ref):
    reopen_modes(x_ref, y_ref)
    for t in range(3):
        m_ref[:, pl.ds(t * 128, 128)] = y_ref[t].astype(bf16)
    for block in range(4):
        rows = pl.ds(block * 256, 256)
        spatial = dot(g_ref[rows, :], m_ref[...])
        h_ref[rows, :] = state_ref[rows, :].astype(f32) + jax.nn.gelu(spatial)
    row = iota((8, 128), 0)
    for q in range(16):
        inner, halo = [], []
        for t in range(3):
            lanes = pl.ds(t * 128, 128)
            inner.append(h_ref[pl.ds(q * 64, 64), lanes])
            right = h_ref[pl.ds((q + 1) % 16 * 64, 1), lanes]
            left = h_ref[pl.ds((q * 64 + 1023) % 1024, 1), lanes]
            halo.append(jnp.where(row == 0, right, jnp.where(row == 1, left, 0.0)))
        first, last = close_cells(*inner)
        first_halo, last_halo = close(*halo)
        rest = pltpu.roll(halo[1], 64, 1)
        first_halo = jnp.where(row == 2, pltpu.roll(rest, 2, 0), first_halo)
        last_halo = jnp.where(row == 2, pltpu.roll(rest, 1, 0), last_halo)
        s_ref[q, :, 0:128] = jnp.concatenate([first, first_halo], axis=0).astype(bf16)
        s_ref[q, :, 128:256] = jnp.concatenate([last, last_halo], axis=0).astype(bf16)


def with_sides(inner, halo):
    return jnp.concatenate([inner, halo, pltpu.roll(halo, 6, 0)], axis=0).astype(bf16)


def tail_weights_kernel(u_ref, w_ref, o_ref, c_ref):
    o_ref[...] = jnp.zeros(o_ref.shape, bf16)
    row, col = iota((1024, 256), 0), iota((1024, 256), 1)
    for q in range(4):
        pick = jnp.where(row == 16 * (col % 64) + 4 * (col // 64) + q, 1.0, 0.0).astype(bf16)
        part = dot(u_ref[...], pick).astype(bf16)
        for b in range(4):
            o_ref[pl.ds(b * 128, 96), pl.ds(q * 256, 256)] = part[b * 96 : (b + 1) * 96]
    for ds in range(3):
        for p in range(4):
            blocks = []
            for window in (0, 1, 2, 3, 4, -1):
                dr = window - p
                if -1 <= dr <= 1:
                    blocks.append(w_ref[3 * (dr + 1) + ds].astype(f32))
                else:
                    blocks.append(jnp.zeros((64, 64), f32))
            c_ref[ds, pl.ds(p * 64, 64), :] = jnp.concatenate(blocks, axis=1).astype(bf16)


def fine_kernel(x_ref, u_ref, bias_ref, o_ref, h_ref):
    row = iota((8, 128), 0)
    for a in range(4):
        for b in range(4):
            cells = x_ref[a * 4 + b].astype(f32)
            first, last = cells[:, 0:128], cells[:, 128:256]
            first_halo, last_halo = first[72:80], last[72:80]
            rest = jnp.where(
                row == 0,
                pltpu.roll(pltpu.roll(first_halo, 64, 1), 6, 0),
                pltpu.roll(pltpu.roll(last_halo, 64, 1), 7, 0),
            )
            tiles = (
                (first[:64], first_halo),
                (reopen_cells(first, last), reopen(first_halo, last_halo, rest)),
                (last[:64], last_halo),
            )
            for t, (inner, halo) in enumerate(tiles):
                h_ref[pl.ds((a * 3 + t) * 80, 80), pl.ds(b * 128, 128)] = with_sides(inner, halo)
    for q in range(4):
        lanes = pl.ds(q * 256, 256)
        for block in range(4):
            rows = pl.ds(block * 240, 240)
            value = dot(h_ref[rows, :], u_ref[:, lanes]) + bias_ref[:, lanes]
            o_ref[q, rows, :] = jax.nn.gelu(value).astype(bf16)


def conv_kernel(
    ends_ref, f_ref, up_ref, down_ref, u_ref, bias_ref, w_ref, cb_ref, o_ref,
    h_ref, e_ref, t_ref, s_ref, z_ref, g_ref,
):
    for b in range(4):
        lanes = pl.ds(b * 128, 128)
        for side, ref in enumerate((up_ref, down_ref)):
            cells = ref[b].astype(f32)
            h_ref[pl.ds(side * 80, 80), lanes] = with_sides(cells[:64], cells[72:80])
    first = iota((160, 256), 0) < 80
    keep = jnp.where(first, ends_ref[0], ends_ref[1]) > 0
    half = iota((80, 128), 1) < 64
    for q in range(4):
        lanes = pl.ds(q * 256, 256)
        value = jax.nn.gelu(dot(h_ref[...], u_ref[:, lanes]) + bias_ref[:, lanes])
        e_ref[...] = jnp.where(keep, value, 0.0).astype(bf16)
        for a in range(12):
            below = e_ref[pl.ds(80, 80), 0:128] if a == 11 else f_ref[q, pl.ds(a * 80 + 80, 80), 0:128]
            above = e_ref[pl.ds(0, 80), 128:256] if a == 0 else f_ref[q, pl.ds(a * 80 - 80, 80), 128:256]
            t_ref[q, pl.ds(a * 80, 80), :] = jnp.where(half, below, above)
    for side, q, amount in ((0, 3, 1), (1, 0, 79)):
        for a in range(12):
            rows = pl.ds(a * 80, 80)
            for t in range(3):
                part = t_ref[q, rows, :] if t == 2 else f_ref[q, rows, t * 128 : (t + 1) * 128]
                s_ref[side, rows, pl.ds(t * 128, 128)] = pltpu.roll(
                    part.astype(f32), amount, 0
                ).astype(bf16)
    for q in range(4):
        total = f_ref[q].astype(f32) + cb_ref[...]
        for ds in range(3):
            source = q + ds - 1
            if 0 <= source < 4:
                total = total + dot_nt(f_ref[source], w_ref[ds, :, 0:256])
                total = total + dot_nt(t_ref[source], w_ref[ds, :, 256:384])
            else:
                total = total + dot_nt(s_ref[0 if source < 0 else 1], w_ref[ds])
        z_ref[q] = total.astype(bf16)
    row, col = iota((256, 256), 0), iota((256, 256), 1)
    place = jnp.where(col == 4 * (row % 64) + row // 64, 1.0, 0.0).astype(bf16)
    for a in range(12):
        cells = jnp.concatenate([z_ref[q, pl.ds(a * 80, 64), :] for q in range(4)], axis=0)
        lines = lax.dot_general(cells, place, (((0,), (0,)), ((), ())), preferred_element_type=f32)
        for p in range(4):
            for t in range(2):
                g_ref[t, pl.ds(4 * a + p, 64, stride=48), :] = lines[
                    p * 64 : (p + 1) * 64, t * 128 : (t + 1) * 128
                ]
    for t in range(2):
        o_ref[:, :, pl.ds(t * 128, 128)] = g_ref[t].reshape(64, 48, 128).astype(bf16)


def start_logs(degrees):
    values = []
    total = 0.0
    for m in range(degrees):
        if m > 0:
            total = total + math.log((2.0 * m - 1.0) / (2.0 * m))
        values.append(0.5 * (math.log((2.0 * m + 1.0) / (4.0 * math.pi)) + total))
    return values


def legendre_tables(n):
    order = 3 * n + jnp.arange(8, dtype=jnp.int32)
    lane = jnp.arange(384, dtype=jnp.int32)
    colatitude = ((3 * (lane % 128) + lane // 128).astype(f32) + 0.5) * (math.pi / 384)
    cosine = jnp.broadcast_to(jnp.cos(colatitude)[None, :], (8, 384))
    log_sine = jnp.log(jnp.sin(colatitude))[None, :]
    logs = jnp.asarray(start_logs(384), f32)
    log_base = jnp.sum(jnp.where(order[:, None] == lane[None, :], logs[None, :], 0.0), axis=1)
    log_start = log_base[:, None] + order.astype(f32)[:, None] * log_sine
    start = jnp.where(log_start > -80.0, jnp.exp(jnp.maximum(log_start, -80.0)), 0.0)
    orders = jnp.broadcast_to(order.astype(f32)[:, None], (8, 128))
    return call(
        legendre_tables_kernel,
        (shape((3, 384, 384)), shape((3, 384, 384))),
        orders,
        cosine,
        start,
        scratch=[pltpu.VMEM((3, 3072, 128), f32)],
        flops=4 * 10**9,
    )


def dft_tables():
    step = 2.0 * math.pi / 1024

    def base(row_axis, dims):
        k, y = iota(dims, row_axis), iota(dims, 1 - row_axis)
        j = k % 8
        wave = 3 * (k // 8) + j % 3
        used = j < 6
        angle = ((wave * y + jnp.where(j < 3, 0, 256)) % 1024).astype(f32) * step
        scale = jnp.where(used, 1.0, 0.0)
        if row_axis == 1:
            scale = scale * jnp.where(wave == 0, 1.0, 2.0)
        turn = (wave * y % 8).astype(f32) * (math.pi / 4)
        return jnp.cos(angle) * scale, jnp.sin(angle) * scale, turn

    p, q, _ = base(0, (1024, 128))
    turn = base(0, (1024, 8))[2]
    pt, qt, _ = base(1, (128, 1024))
    turn_t = base(1, (8, 1024))[2]
    return call(
        dft_tables_kernel,
        (shape((1024, 1024)), shape((1024, 1024))),
        p, q, jnp.cos(turn), jnp.sin(turn), pt, qt, jnp.cos(turn_t), jnp.sin(turn_t),
        flops=4 * 10**9,
    )


def exchange(x, axes):
    return lax.all_to_all(x, axes, 0, 0, tiled=True)


def local(state_field, mix_weight, upsample_weight, upsample_bias, conv_weight, conv_bias):
    lat = lax.axis_index("lat")
    n = 4 * lat + lax.axis_index("qa")
    own_degrees = exchange(mix_weight, "qb")
    gathered = lax.all_gather(own_degrees, "qa", axis=0).reshape(16, 3, 24, 384)
    packed = call(pack_kernel, shape((16, 72, 256)), state_field, flops=10**9)
    arrived = exchange(packed, ("qa", "qb"))
    forward, inverse = dft_tables()
    colatitude = ((3 * n + jnp.arange(384, dtype=jnp.int32) // 128).astype(f32) + 0.5) * (
        math.pi / 384
    )
    scale = (jnp.sin(colatitude) * (math.pi / 384) * (2.0 * math.pi / 1024))[None, :]
    scratch = [pltpu.VMEM((3, 1024, 128), f32)] * 2
    spectra, state = call(
        dft_kernel,
        (shape((1024, 256)), shape((1024, 384))),
        forward,
        arrived,
        scale,
        scratch=scratch[:1],
        flops=10**9,
    )
    columns = exchange(spectra, ("lat", "qa"))
    basis, basis_t = legendre_tables(n)
    coeffs = call(legendre_kernel, shape((1024, 256)), columns, basis, scratch=scratch, flops=10**9)
    degrees = exchange(coeffs, ("lat", "qb"))
    mixer = spread_mix_weight(gathered)
    mixed = call(mix_kernel, shape((1024, 256)), degrees, mixer, scratch=scratch, flops=10**9)
    returned = exchange(mixed, ("lat", "qb"))
    synthesized = call(
        legendre_kernel, shape((1024, 256)), returned, basis_t, scratch=scratch, flops=10**9
    )
    modes = exchange(synthesized, ("lat", "qa"))
    hidden = call(
        inverse_kernel,
        shape((16, 80, 256)),
        inverse,
        modes,
        state,
        scratch=[scratch[0], pltpu.VMEM((1024, 384), bf16), pltpu.VMEM((1024, 384), f32)],
        flops=10**9,
    )
    cells = exchange(hidden, ("qa", "qb"))
    spread_up, spread_conv = call(
        tail_weights_kernel,
        (shape((512, 1024)), shape((3, 256, 384))),
        upsample_weight,
        conv_weight,
        flops=2 * 10**9,
    )
    first_row = cells[0:4, :, 0:128]
    last_row = cells[12:16, :, 128:256]
    count = lax.axis_size("lat")
    up = lax.ppermute(last_row, "lat", [(i, i + 1) for i in range(count - 1)])
    down = lax.ppermute(first_row, "lat", [(i + 1, i) for i in range(count - 1)])
    bias = jnp.tile(upsample_bias, 16)[None, :]
    fine = call(
        fine_kernel,
        shape((4, 960, 256)),
        cells,
        spread_up,
        bias,
        scratch=[pltpu.VMEM((960, 512), bf16)],
        flops=10**10,
    )
    ends = jnp.stack([lat > 0, lat < count - 1]).astype(jnp.int32)
    return call(
        conv_kernel,
        shape((64, 48, 256)),
        ends,
        fine,
        up,
        down,
        spread_up,
        bias,
        spread_conv,
        jnp.tile(conv_bias, 4)[None, :],
        smem=(0,),
        scratch=[
            pltpu.VMEM((160, 512), bf16),
            pltpu.VMEM((160, 256), bf16),
            pltpu.VMEM((4, 960, 128), bf16),
            pltpu.VMEM((2, 960, 384), bf16),
            pltpu.VMEM((4, 960, 256), bf16),
            pltpu.VMEM((2, 3072, 128), f32),
        ],
        flops=10**10,
    )


def solution(mesh):
    fine_mesh = Mesh(mesh.devices.reshape(32, 4, 4), ("lat", "qa", "qb"))
    rows = P("lat", ("qa", "qb"), None)
    return jax.shard_map(
        local,
        mesh=fine_mesh,
        in_specs=(rows, rows, P(), P(), P(), P()),
        out_specs=P(None, "lat", ("qa", "qb")),
        check_vma=False,
    )
```

```python
import math

import jax
import jax.numpy as jnp
from jax import lax
from jax.experimental import pallas as pl
from jax.experimental.pallas import tpu as pltpu
from jax.sharding import Mesh
from jax.sharding import PartitionSpec as P

f32 = jnp.float32
bf16 = jnp.bfloat16
MIB = 1 << 20


def call(kernel, out, *args, scratch=(), flops=0, smem=(), vmem=40):
    space = [
        pl.BlockSpec(memory_space=pltpu.SMEM if i in smem else pltpu.VMEM) for i in range(len(args))
    ]
    outs = out if isinstance(out, (tuple, list)) else (out,)
    moved = sum(x.size * x.dtype.itemsize for x in (*args, *outs))
    return pl.pallas_call(
        kernel,
        out_shape=out,
        in_specs=space,
        out_specs=jax.tree.map(lambda _: pl.BlockSpec(memory_space=pltpu.VMEM), out),
        scratch_shapes=list(scratch),
        compiler_params=pltpu.CompilerParams(vmem_limit_bytes=vmem * MIB),
        cost_estimate=pl.CostEstimate(flops=flops, bytes_accessed=moved, transcendentals=0),
    )(*args)


def shape(dims, dtype=bf16):
    return jax.ShapeDtypeStruct(dims, dtype)


def iota(dims, axis):
    return lax.broadcasted_iota(jnp.int32, dims, axis)


def widen():
    row, col = iota((384, 512), 0), iota((384, 512), 1)
    return jnp.where((col % 128 < 96) & (row == col // 128 * 96 + col % 128), 1.0, 0.0).astype(bf16)


def dot(a, b):
    return jnp.dot(a, b, preferred_element_type=f32)


def dot_nt(a, b):
    return lax.dot_general(a, b, (((1,), (1,)), ((), ())), preferred_element_type=f32)


def lanes_of(x):
    return iota(x.shape, 1)


def close(first, middle, last):
    lane = lanes_of(first)
    return (
        jnp.where(lane < 96, first, pltpu.roll(middle, 96, 1)),
        jnp.where(lane < 96, last, pltpu.roll(middle, 64, 1)),
    )


def reopen(first, last, rest):
    lane = lanes_of(first)
    return jnp.where(
        lane < 32, pltpu.roll(first, 32, 1), jnp.where(lane < 64, pltpu.roll(last, 64, 1), rest)
    )


def side_by_side(parts):
    group = lanes_of(parts[0]) // 32
    total = jnp.zeros(parts[0].shape, f32)
    for i, part in enumerate(parts):
        total = jnp.where(group == i, pltpu.roll(part, (32 * i + 64) % 128, 1), total)
    return total


def apart(x, i):
    return pltpu.roll(x, (64 - 32 * i) % 128, 1)


def close_cells(first, middle, last):
    a, b = close(first, middle, last)
    pieces = [middle[8 * g : 8 * g + 8] for g in range(8)]
    return (
        jnp.concatenate([a, side_by_side(pieces[:4])], axis=0),
        jnp.concatenate([b, side_by_side(pieces[4:])], axis=0),
    )


def reopen_cells(first, last):
    rest = [apart(first[64:72], i) for i in range(4)] + [apart(last[64:72], i) for i in range(4)]
    return reopen(first[:64], last[:64], jnp.concatenate(rest, axis=0))


def mode_row(j):
    return pl.ds(j, 128, stride=8)


def close_modes(y_ref, s_ref):
    a, b = close(y_ref[0], y_ref[1], y_ref[2])
    y_ref[0], y_ref[2] = a, b
    y_ref[0, mode_row(6), :] = side_by_side([y_ref[1, mode_row(j), :] for j in range(4)])
    y_ref[2, mode_row(6), :] = side_by_side([y_ref[1, mode_row(j), :] for j in range(4, 6)])
    s_ref[:, 0:128] = y_ref[0].astype(bf16)
    s_ref[:, 128:256] = y_ref[2].astype(bf16)


def reopen_modes(x_ref, y_ref):
    first, last = x_ref[:, 0:128].astype(f32), x_ref[:, 128:256].astype(f32)
    y_ref[0], y_ref[2] = first, last
    y_ref[1] = reopen(first, last, jnp.zeros(first.shape, f32))
    rest = y_ref[0, mode_row(6), :], y_ref[2, mode_row(6), :]
    upper = lanes_of(rest[0]) >= 64
    for j in range(6):
        y_ref[1, mode_row(j), :] = jnp.where(
            upper, apart(rest[j // 4], j % 4), y_ref[1, mode_row(j), :]
        )


def weight_tile(r, og, it):
    index = r * 9 + og * 3 + it
    return index // 7, index % 7


def pack_kernel(x_ref, w_ref, s_ref):
    spread = widen()
    blank = jnp.zeros((8, 128), f32)
    for a in range(4):
        wide = [dot(x_ref[3 * a + t], spread) for t in range(3)]
        for b in range(4):
            first, last = close_cells(*(w[:, b * 128 : (b + 1) * 128] for w in wide))
            tiles = {}
            for r in range(3):
                weights = w_ref[3 * b + r].astype(f32)
                for og in range(3):
                    for it in range(3):
                        tiles[weight_tile(r, og, it)] = weights[
                            8 * og : 8 * og + 8, 128 * it : 128 * it + 128
                        ]
            for side, cells in enumerate((first, last)):
                parts = [tiles.get((a, 2 * row + side), blank) for row in range(4)]
                s_ref[a * 4 + b, :, pl.ds(side * 128, 128)] = jnp.concatenate(
                    [cells, *parts], axis=0
                ).astype(bf16)


def dft_tables_kernel(p_ref, q_ref, cb_ref, sb_ref, pt_ref, qt_ref, cbt_ref, sbt_ref, c_ref, g_ref):
    for b in range(8):
        c_ref[:, pl.ds(b * 128, 128)] = (
            p_ref[...] * cb_ref[:, b : b + 1] - q_ref[...] * sb_ref[:, b : b + 1]
        ).astype(bf16)
        g_ref[pl.ds(b * 128, 128), :] = (
            pt_ref[...] * cbt_ref[b : b + 1, :] - qt_ref[...] * sbt_ref[b : b + 1, :]
        ).astype(bf16)


def dft_kernel(c_ref, x_ref, w_ref, s_ref, state_ref, part_ref, y_ref):
    for q in range(16):
        cells = x_ref[q].astype(f32)
        first, last = cells[:, 0:128], cells[:, 128:256]
        rows = pl.ds(q * 64, 64)
        state_ref[rows, 0:128] = first[:64].astype(bf16)
        state_ref[rows, 128:256] = reopen_cells(first, last).astype(bf16)
        state_ref[rows, 256:384] = last[:64].astype(bf16)
        parts = [
            cells[72 + i // 2 * 8 : 80 + i // 2 * 8, i % 2 * 128 : i % 2 * 128 + 128]
            for i in range(7)
        ]
        part_ref[q] = jnp.concatenate(parts, axis=0).astype(bf16)
    for block in range(4):
        rows = pl.ds(block * 256, 256)
        result = dot(c_ref[rows, :], state_ref[...]) * w_ref[...]
        for t in range(3):
            y_ref[t, rows, :] = result[:, t * 128 : (t + 1) * 128]
    close_modes(y_ref, s_ref)


def legendre_tables_kernel(order_ref, cosine_ref, start_ref, l_ref, t_ref, rows_ref):
    order = order_ref[...]
    squared = order * order
    rows_ref[...] = jnp.zeros(rows_ref.shape, f32)

    def step(l, carry):
        previous, earlier = carry
        degree = l.astype(f32)
        above = degree > order
        spacing = jnp.where(above, degree * degree - squared, 1.0)
        alpha = jnp.where(
            above, jnp.sqrt(jnp.maximum(4.0 * degree * degree - 1.0, 1.0) / spacing), 0.0
        )
        below = degree - 1.0
        beta = jnp.where(
            degree > order + 1.0,
            jnp.sqrt(
                jnp.maximum(below * below - squared, 0.0)
                / jnp.maximum(4.0 * below * below - 1.0, 1.0)
            ),
            0.0,
        )
        first = degree == order
        current = []
        for t in range(3):
            lanes = pl.ds(t * 128, 128)
            value = alpha * (cosine_ref[:, lanes] * previous[t] - beta * earlier[t]) + jnp.where(
                first, start_ref[:, lanes], 0.0
            )
            rows_ref[t, pl.ds(pl.multiple_of(l * 8, 8), 8), :] = value
            current.append(value)
        return (tuple(current), previous)

    zeros = (jnp.zeros((8, 128), f32),) * 3

    def block(i, carry):
        for u in range(8):
            carry = step(i * 8 + u, carry)
        return carry

    lax.fori_loop(0, 48, block, (zeros, zeros))
    for m3 in range(3):
        for t in range(3):
            parts = [rows_ref[t, pl.ds(r * 8 + m3, 128, stride=24), :] for r in range(3)]
            table = jnp.concatenate(parts, axis=0)
            l_ref[m3, :, pl.ds(t * 128, 128)] = table.astype(bf16)
            t_ref[m3, pl.ds(t * 128, 128), :] = table.T.astype(bf16)


def legendre_kernel(x_ref, l_ref, s_ref, in_ref, out_ref):
    reopen_modes(x_ref, in_ref)
    out_ref[...] = jnp.zeros(out_ref.shape, f32)
    for m3 in range(3):
        halves = [
            jnp.concatenate(
                [in_ref[t, pl.ds(cs * 3 + m3, 128, stride=8), :] for t in range(3)], axis=0
            )
            for cs in range(2)
        ]
        result = dot(l_ref[m3], jnp.concatenate(halves, axis=1).astype(bf16))
        for t in range(3):
            for cs in range(2):
                out_ref[t, pl.ds(cs * 3 + m3, 128, stride=8), :] = result[
                    t * 128 : (t + 1) * 128, cs * 128 : (cs + 1) * 128
                ]
    close_modes(out_ref, s_ref)


def mix_weight_kernel(w_ref, o_ref, full_ref):
    spread = widen()
    o_ref[...] = jnp.zeros(o_ref.shape, bf16)
    for r in range(3):
        for og in range(3):
            for it in range(3):
                a, i = weight_tile(r, og, it)
                full_ref[:, og, :, pl.ds(it * 128, 128)] = w_ref[a].astype(f32)[
                    :, 8 * i : 8 * i + 8
                ]
        part = full_ref[...].reshape(384, 384).astype(bf16)
        wide = dot(part, spread).astype(bf16)
        for b in range(4):
            o_ref[r, pl.ds(b * 128, 96), :] = wide[b * 96 : (b + 1) * 96]


def mix_kernel(x_ref, w_ref, s_ref, in_ref, out_ref):
    reopen_modes(x_ref, in_ref)
    for r in range(3):
        part = in_ref[r].reshape(32, 4, 8, 128)
        modes = jnp.concatenate([part[:, b].reshape(256, 128) for b in range(4)], axis=1)
        mixed = dot_nt(modes.astype(bf16), w_ref[r])
        back = [mixed[:, b * 128 : (b + 1) * 128].reshape(32, 1, 8, 128) for b in range(4)]
        out_ref[r] = jnp.concatenate(back, axis=1).reshape(1024, 128)
    close_modes(out_ref, s_ref)


def inverse_kernel(g_ref, x_ref, state_ref, s_ref, y_ref, m_ref, h_ref):
    reopen_modes(x_ref, y_ref)
    for t in range(3):
        m_ref[:, pl.ds(t * 128, 128)] = y_ref[t].astype(bf16)
    for block in range(4):
        rows = pl.ds(block * 256, 256)
        spatial = dot(g_ref[rows, :], m_ref[...])
        h_ref[rows, :] = state_ref[rows, :].astype(f32) + jax.nn.gelu(spatial)
    row = iota((8, 128), 0)
    for q in range(16):
        inner, halo = [], []
        for t in range(3):
            lanes = pl.ds(t * 128, 128)
            inner.append(h_ref[pl.ds(q * 64, 64), lanes])
            right = h_ref[pl.ds((q + 1) % 16 * 64, 1), lanes]
            left = h_ref[pl.ds((q * 64 + 1023) % 1024, 1), lanes]
            halo.append(jnp.where(row == 0, right, jnp.where(row == 1, left, 0.0)))
        first, last = close_cells(*inner)
        first_halo, last_halo = close(*halo)
        rest = pltpu.roll(halo[1], 64, 1)
        first_halo = jnp.where(row == 2, pltpu.roll(rest, 2, 0), first_halo)
        last_halo = jnp.where(row == 2, pltpu.roll(rest, 1, 0), last_halo)
        s_ref[q, :, 0:128] = jnp.concatenate([first, first_halo], axis=0).astype(bf16)
        s_ref[q, :, 128:256] = jnp.concatenate([last, last_halo], axis=0).astype(bf16)


def with_sides(inner, halo):
    return jnp.concatenate([inner, halo, pltpu.roll(halo, 6, 0)], axis=0).astype(bf16)


def tail_weights_kernel(u_ref, w_ref, o_ref, c_ref):
    o_ref[...] = jnp.zeros(o_ref.shape, bf16)
    row, col = iota((1024, 256), 0), iota((1024, 256), 1)
    for q in range(4):
        pick = jnp.where(row == 16 * (col % 64) + 4 * (col // 64) + q, 1.0, 0.0).astype(bf16)
        part = dot(u_ref[...], pick).astype(bf16)
        for b in range(4):
            o_ref[pl.ds(b * 128, 96), pl.ds(q * 256, 256)] = part[b * 96 : (b + 1) * 96]
    for p in range(4):
        blocks = []
        for ds in range(3):
            for window in (0, 1, 2, 3, 4, -1):
                dr = window - p
                if -1 <= dr <= 1:
                    blocks.append(w_ref[3 * (dr + 1) + ds].astype(f32))
                else:
                    blocks.append(jnp.zeros((64, 64), f32))
        c_ref[pl.ds(p * 64, 64), :] = jnp.concatenate(blocks, axis=1).astype(bf16)


def fine_kernel(x_ref, u_ref, bias_ref, o_ref, side_ref, h_ref):
    row = iota((8, 128), 0)
    for a in range(4):
        for b in range(4):
            cells = x_ref[a * 4 + b].astype(f32)
            first, last = cells[:, 0:128], cells[:, 128:256]
            first_halo, last_halo = first[72:80], last[72:80]
            rest = jnp.where(
                row == 0,
                pltpu.roll(pltpu.roll(first_halo, 64, 1), 6, 0),
                pltpu.roll(pltpu.roll(last_halo, 64, 1), 7, 0),
            )
            tiles = (
                (first[:64], first_halo),
                (reopen_cells(first, last), reopen(first_halo, last_halo, rest)),
                (last[:64], last_halo),
            )
            for t, (inner, halo) in enumerate(tiles):
                h_ref[pl.ds((a * 3 + t) * 80, 80), pl.ds(b * 128, 128)] = with_sides(inner, halo)
    for q in range(4):
        lanes = pl.ds(q * 256, 256)
        for block in range(4):
            rows = pl.ds(block * 240, 240)
            value = dot(h_ref[rows, :], u_ref[:, lanes]) + bias_ref[:, lanes]
            value = jax.nn.gelu(value).astype(bf16)
            for i in range(3):
                a = block * 3 + i
                o_ref[q, pl.ds(a * 64, 64), :] = value[i * 80 : i * 80 + 64]
                side_ref[q, pl.ds(a * 16, 16), :] = value[i * 80 + 64 : i * 80 + 80]


def conv_kernel(
    ends_ref, f_ref, side_ref, up_ref, down_ref, u_ref, bias_ref, w_ref, cb_ref, o_ref,
    h_ref, e_ref, t_ref, s_ref, z_ref, g_ref,
):
    for b in range(4):
        lanes = pl.ds(b * 128, 128)
        for side, ref in enumerate((up_ref, down_ref)):
            cells = ref[b].astype(f32)
            h_ref[pl.ds(side * 80, 80), lanes] = with_sides(cells[:64], cells[72:80])
    keep = jnp.where(iota((160, 256), 0) < 80, ends_ref[0], ends_ref[1]) > 0

    def around(q, ref, a, size, start):
        half = iota((size, 128), 1) < 64
        below = e_ref[pl.ds(80 + start, size), 0:128]
        above = e_ref[pl.ds(start, size), 128:256]
        if a < 11:
            below = ref[q, pl.ds((a + 1) * size, size), 0:128]
        if a > 0:
            above = ref[q, pl.ds((a - 1) * size, size), 128:256]
        return jnp.where(half, below, above)

    for q in range(4):
        lanes = pl.ds(q * 256, 256)
        value = jax.nn.gelu(dot(h_ref[...], u_ref[:, lanes]) + bias_ref[:, lanes])
        e_ref[...] = jnp.where(keep, value, 0.0).astype(bf16)
        for a in range(12):
            rows = pl.ds(a * 64, 64)
            outer = around(q, f_ref, a, 64, 0)
            t_ref[q, rows, :] = outer
            if q in (0, 3):
                side, amount = (0, 1) if q == 3 else (1, 79)
                edges = pl.ds(a * 16, 16)
                for t in range(3):
                    if t < 2:
                        inner = f_ref[q, rows, t * 128 : (t + 1) * 128]
                        edge = side_ref[q, edges, t * 128 : (t + 1) * 128]
                    else:
                        inner, edge = outer, around(q, side_ref, a, 16, 64)
                    column = jnp.concatenate([inner, edge], axis=0).astype(f32)
                    column = pltpu.roll(column, amount, 0)[:64]
                    s_ref[side, rows, pl.ds(t * 128, 128)] = column.astype(bf16)
    for q in range(4):
        parts = []
        for source in (q - 1, q, q + 1):
            if 0 <= source < 4:
                parts += [f_ref[source], t_ref[source]]
            else:
                parts.append(s_ref[0 if source < 0 else 1])
        total = dot_nt(jnp.concatenate(parts, axis=1), w_ref[...])
        z_ref[q] = (total + f_ref[q].astype(f32) + cb_ref[...]).astype(bf16)
    row, col = iota((256, 256), 0), iota((256, 256), 1)
    place = jnp.where(col == 4 * (row % 64) + row // 64, 1.0, 0.0).astype(bf16)
    for a in range(12):
        cells = jnp.concatenate([z_ref[q, pl.ds(a * 64, 64), :] for q in range(4)], axis=0)
        lines = lax.dot_general(cells, place, (((0,), (0,)), ((), ())), preferred_element_type=f32)
        for p in range(4):
            for t in range(2):
                g_ref[t, pl.ds(4 * a + p, 64, stride=48), :] = lines[
                    p * 64 : (p + 1) * 64, t * 128 : (t + 1) * 128
                ]
    for t in range(2):
        o_ref[:, :, pl.ds(t * 128, 128)] = g_ref[t].reshape(64, 48, 128).astype(bf16)


def start_logs(degrees):
    values = []
    total = 0.0
    for m in range(degrees):
        if m > 0:
            total = total + math.log((2.0 * m - 1.0) / (2.0 * m))
        values.append(0.5 * (math.log((2.0 * m + 1.0) / (4.0 * math.pi)) + total))
    return values


def legendre_tables(n):
    order = 3 * n + jnp.arange(8, dtype=jnp.int32)
    lane = jnp.arange(384, dtype=jnp.int32)
    colatitude = ((3 * (lane % 128) + lane // 128).astype(f32) + 0.5) * (math.pi / 384)
    cosine = jnp.broadcast_to(jnp.cos(colatitude)[None, :], (8, 384))
    log_sine = jnp.log(jnp.sin(colatitude))[None, :]
    logs = jnp.asarray(start_logs(384), f32)
    log_base = jnp.sum(jnp.where(order[:, None] == lane[None, :], logs[None, :], 0.0), axis=1)
    log_start = log_base[:, None] + order.astype(f32)[:, None] * log_sine
    start = jnp.where(log_start > -80.0, jnp.exp(jnp.maximum(log_start, -80.0)), 0.0)
    orders = jnp.broadcast_to(order.astype(f32)[:, None], (8, 128))
    return call(
        legendre_tables_kernel,
        (shape((3, 384, 384)), shape((3, 384, 384))),
        orders,
        cosine,
        start,
        scratch=[pltpu.VMEM((3, 3072, 128), f32)],
        flops=4 * 10**9,
    )


def dft_tables():
    step = 2.0 * math.pi / 1024

    def base(row_axis, dims):
        k, y = iota(dims, row_axis), iota(dims, 1 - row_axis)
        j = k % 8
        wave = 3 * (k // 8) + j % 3
        used = j < 6
        angle = ((wave * y + jnp.where(j < 3, 0, 256)) % 1024).astype(f32) * step
        scale = jnp.where(used, 1.0, 0.0)
        if row_axis == 1:
            scale = scale * jnp.where(wave == 0, 1.0, 2.0)
        turn = (wave * y % 8).astype(f32) * (math.pi / 4)
        return jnp.cos(angle) * scale, jnp.sin(angle) * scale, turn

    p, q, _ = base(0, (1024, 128))
    turn = base(0, (1024, 8))[2]
    pt, qt, _ = base(1, (128, 1024))
    turn_t = base(1, (8, 1024))[2]
    return call(
        dft_tables_kernel,
        (shape((1024, 1024)), shape((1024, 1024))),
        p, q, jnp.cos(turn), jnp.sin(turn), pt, qt, jnp.cos(turn_t), jnp.sin(turn_t),
        flops=4 * 10**9,
    )


def exchange(x, axes):
    return lax.all_to_all(x, axes, 0, 0, tiled=True)


def local(state_field, mix_weight, upsample_weight, upsample_bias, conv_weight, conv_bias):
    lat = lax.axis_index("lat")
    n = 4 * lat + lax.axis_index("qa")
    packed = call(pack_kernel, shape((16, 104, 256)), state_field, mix_weight, flops=10**9)
    arrived = exchange(packed, ("qa", "qb"))
    forward, inverse = dft_tables()
    colatitude = ((3 * n + jnp.arange(384, dtype=jnp.int32) // 128).astype(f32) + 0.5) * (
        math.pi / 384
    )
    scale = (jnp.sin(colatitude) * (math.pi / 384) * (2.0 * math.pi / 1024))[None, :]
    scratch = [pltpu.VMEM((3, 1024, 128), f32)] * 2
    spectra, state, own = call(
        dft_kernel,
        (shape((1024, 256)), shape((1024, 384)), shape((16, 56, 128))),
        forward,
        arrived,
        scale,
        scratch=scratch[:1],
        flops=10**9,
    )
    columns = exchange(spectra, ("lat", "qa"))
    basis, basis_t = legendre_tables(n)
    coeffs = call(legendre_kernel, shape((1024, 256)), columns, basis, scratch=scratch, flops=10**9)
    spread_up, spread_conv = call(
        tail_weights_kernel,
        (shape((512, 1024)), shape((256, 1152))),
        upsample_weight,
        conv_weight,
        flops=2 * 10**9,
    )
    coeffs, spread_up, spread_conv = lax.optimization_barrier((coeffs, spread_up, spread_conv))
    degrees = exchange(coeffs, ("lat", "qb"))
    gathered = lax.all_gather(own, "qa", axis=0)
    mixer = call(
        mix_weight_kernel,
        shape((3, 512, 512)),
        gathered,
        scratch=[pltpu.VMEM((16, 3, 8, 384), f32)],
        flops=10**9,
    )
    mixed = call(mix_kernel, shape((1024, 256)), degrees, mixer, scratch=scratch, flops=10**9)
    returned = exchange(mixed, ("lat", "qb"))
    synthesized = call(
        legendre_kernel, shape((1024, 256)), returned, basis_t, scratch=scratch, flops=10**9
    )
    modes = exchange(synthesized, ("lat", "qa"))
    hidden = call(
        inverse_kernel,
        shape((16, 80, 256)),
        inverse,
        modes,
        state,
        scratch=[scratch[0], pltpu.VMEM((1024, 384), bf16), pltpu.VMEM((1024, 384), f32)],
        flops=10**9,
    )
    cells = exchange(hidden, ("qa", "qb"))
    first_row = cells[0:4, :, 0:128]
    last_row = cells[12:16, :, 128:256]
    count = lax.axis_size("lat")
    up = lax.ppermute(last_row, "lat", [(i, i + 1) for i in range(count - 1)])
    down = lax.ppermute(first_row, "lat", [(i + 1, i) for i in range(count - 1)])
    bias = jnp.tile(upsample_bias, 16)[None, :]
    fine, sides = call(
        fine_kernel,
        (shape((4, 768, 256)), shape((4, 192, 256))),
        cells,
        spread_up,
        bias,
        scratch=[pltpu.VMEM((960, 512), bf16)],
        flops=10**10,
    )
    ends = jnp.stack([lat > 0, lat < count - 1]).astype(jnp.int32)
    return call(
        conv_kernel,
        shape((64, 48, 256)),
        ends,
        fine,
        sides,
        up,
        down,
        spread_up,
        bias,
        spread_conv,
        jnp.tile(conv_bias, 4)[None, :],
        smem=(0,),
        scratch=[
            pltpu.VMEM((160, 512), bf16),
            pltpu.VMEM((160, 256), bf16),
            pltpu.VMEM((4, 768, 128), bf16),
            pltpu.VMEM((2, 768, 384), bf16),
            pltpu.VMEM((4, 768, 256), bf16),
            pltpu.VMEM((2, 3072, 128), f32),
        ],
        flops=10**10,
    )


def solution(mesh):
    fine_mesh = Mesh(mesh.devices.reshape(32, 4, 4), ("lat", "qa", "qb"))
    rows = P("lat", ("qa", "qb"), None)
    return jax.shard_map(
        local,
        mesh=fine_mesh,
        in_specs=(rows, rows, P(), P(), P(), P()),
        out_specs=P(None, "lat", ("qa", "qb")),
        check_vma=False,
    )
```

```python
import functools
import math

import jax
import jax.numpy as jnp
from jax import lax
from jax.experimental import pallas as pl
from jax.experimental.pallas import tpu as pltpu
from jax.sharding import Mesh
from jax.sharding import PartitionSpec as P

f32 = jnp.float32
bf16 = jnp.bfloat16
MIB = 1 << 20


def call(kernel, out, *args, scratch=(), flops=0, smem=(), vmem=40):
    space = [
        pl.BlockSpec(memory_space=pltpu.SMEM if i in smem else pltpu.VMEM) for i in range(len(args))
    ]
    outs = out if isinstance(out, (tuple, list)) else (out,)
    moved = sum(x.size * x.dtype.itemsize for x in (*args, *outs))
    return pl.pallas_call(
        kernel,
        out_shape=out,
        in_specs=space,
        out_specs=jax.tree.map(lambda _: pl.BlockSpec(memory_space=pltpu.VMEM), out),
        scratch_shapes=list(scratch),
        compiler_params=pltpu.CompilerParams(vmem_limit_bytes=vmem * MIB),
        cost_estimate=pl.CostEstimate(flops=flops, bytes_accessed=moved, transcendentals=0),
    )(*args)


def shape(dims, dtype=bf16):
    return jax.ShapeDtypeStruct(dims, dtype)


def iota(dims, axis):
    return lax.broadcasted_iota(jnp.int32, dims, axis)


def widen():
    row, col = iota((384, 512), 0), iota((384, 512), 1)
    return jnp.where((col % 128 < 96) & (row == col // 128 * 96 + col % 128), 1.0, 0.0).astype(bf16)


def dot(a, b):
    return jnp.dot(a, b, preferred_element_type=f32)


def dot_nt(a, b):
    return lax.dot_general(a, b, (((1,), (1,)), ((), ())), preferred_element_type=f32)


def lanes_of(x):
    return iota(x.shape, 1)


def close(first, middle, last):
    lane = lanes_of(first)
    return (
        jnp.where(lane < 96, first, pltpu.roll(middle, 96, 1)),
        jnp.where(lane < 96, last, pltpu.roll(middle, 64, 1)),
    )


def reopen(first, last, rest):
    lane = lanes_of(first)
    return jnp.where(
        lane < 32, pltpu.roll(first, 32, 1), jnp.where(lane < 64, pltpu.roll(last, 64, 1), rest)
    )


def side_by_side(parts):
    group = lanes_of(parts[0]) // 32
    total = jnp.zeros(parts[0].shape, f32)
    for i, part in enumerate(parts):
        total = jnp.where(group == i, pltpu.roll(part, (32 * i + 64) % 128, 1), total)
    return total


def apart(x, i):
    return pltpu.roll(x, (64 - 32 * i) % 128, 1)


def close_cells(first, middle, last):
    a, b = close(first, middle, last)
    pieces = [middle[8 * g : 8 * g + 8] for g in range(8)]
    return (
        jnp.concatenate([a, side_by_side(pieces[:4])], axis=0),
        jnp.concatenate([b, side_by_side(pieces[4:])], axis=0),
    )


def reopen_cells(first, last):
    rest = [apart(first[64:72], i) for i in range(4)] + [apart(last[64:72], i) for i in range(4)]
    return reopen(first[:64], last[:64], jnp.concatenate(rest, axis=0))


def mode_row(j):
    return pl.ds(j, 128, stride=8)


def close_modes(y_ref, s_ref):
    a, b = close(y_ref[0], y_ref[1], y_ref[2])
    y_ref[0], y_ref[2] = a, b
    y_ref[0, mode_row(6), :] = side_by_side([y_ref[1, mode_row(j), :] for j in range(4)])
    y_ref[2, mode_row(6), :] = side_by_side([y_ref[1, mode_row(j), :] for j in range(4, 6)])
    s_ref[:, 0:128] = y_ref[0].astype(bf16)
    s_ref[:, 128:256] = y_ref[2].astype(bf16)


def reopen_modes(x_ref, y_ref):
    first, last = x_ref[:, 0:128].astype(f32), x_ref[:, 128:256].astype(f32)
    y_ref[0], y_ref[2] = first, last
    y_ref[1] = reopen(first, last, jnp.zeros(first.shape, f32))
    rest = y_ref[0, mode_row(6), :], y_ref[2, mode_row(6), :]
    upper = lanes_of(rest[0]) >= 64
    for j in range(6):
        y_ref[1, mode_row(j), :] = jnp.where(
            upper, apart(rest[j // 4], j % 4), y_ref[1, mode_row(j), :]
        )


def weight_tile(r, og, it):
    index = r * 9 + og * 3 + it
    return index // 7, index % 7


def pack_kernel(x_ref, w_ref, s_ref):
    spread = widen()
    blank = jnp.zeros((8, 128), f32)
    for a in range(4):
        wide = [dot(x_ref[3 * a + t], spread) for t in range(3)]
        for b in range(4):
            first, last = close_cells(*(w[:, b * 128 : (b + 1) * 128] for w in wide))
            tiles = {}
            for r in range(3):
                weights = w_ref[3 * b + r].astype(f32)
                for og in range(3):
                    for it in range(3):
                        tiles[weight_tile(r, og, it)] = weights[
                            8 * og : 8 * og + 8, 128 * it : 128 * it + 128
                        ]
            for side, cells in enumerate((first, last)):
                parts = [tiles.get((a, 2 * row + side), blank) for row in range(4)]
                s_ref[a * 4 + b, :, pl.ds(side * 128, 128)] = jnp.concatenate(
                    [cells, *parts], axis=0
                ).astype(bf16)


def dft_tables_kernel(p_ref, q_ref, cb_ref, sb_ref, pt_ref, qt_ref, cbt_ref, sbt_ref, c_ref, g_ref):
    for b in range(8):
        c_ref[:, pl.ds(b * 128, 128)] = (
            p_ref[...] * cb_ref[:, b : b + 1] - q_ref[...] * sb_ref[:, b : b + 1]
        ).astype(bf16)
    for b in range(4):
        g_ref[pl.ds(b * 128, 128), :] = (
            pt_ref[...] * cbt_ref[b : b + 1, :] - qt_ref[...] * sbt_ref[b : b + 1, :]
        ).astype(bf16)


def dft_kernel(c_ref, x_ref, w_ref, s_ref, state_ref, part_ref, y_ref):
    for q in range(16):
        cells = x_ref[q].astype(f32)
        first, last = cells[:, 0:128], cells[:, 128:256]
        rows = pl.ds(q * 64, 64)
        state_ref[rows, 0:128] = first[:64].astype(bf16)
        state_ref[rows, 128:256] = reopen_cells(first, last).astype(bf16)
        state_ref[rows, 256:384] = last[:64].astype(bf16)
        parts = [
            cells[72 + i // 2 * 8 : 80 + i // 2 * 8, i % 2 * 128 : i % 2 * 128 + 128]
            for i in range(7)
        ]
        part_ref[q] = jnp.concatenate(parts, axis=0).astype(bf16)
    for t in range(3):
        for j in (6, 7):
            y_ref[t, mode_row(j), :] = jnp.zeros((128, 128), f32)
    for block in range(3):
        result = dot(c_ref[pl.ds(block * 256, 256), :], state_ref[...]) * w_ref[...]
        for t in range(3):
            for i in range(2):
                y_ref[t, mode_row(2 * block + i), :] = result[
                    i * 128 : (i + 1) * 128, t * 128 : (t + 1) * 128
                ]
    close_modes(y_ref, s_ref)


def legendre_tables_kernel(order_ref, cosine_ref, start_ref, l_ref, rows_ref):
    order = order_ref[...]
    squared = order * order
    rows_ref[...] = jnp.zeros(rows_ref.shape, f32)

    def step(l, carry):
        previous, earlier = carry
        degree = l.astype(f32)
        above = degree > order
        spacing = jnp.where(above, degree * degree - squared, 1.0)
        alpha = jnp.where(
            above, jnp.sqrt(jnp.maximum(4.0 * degree * degree - 1.0, 1.0) / spacing), 0.0
        )
        below = degree - 1.0
        beta = jnp.where(
            degree > order + 1.0,
            jnp.sqrt(
                jnp.maximum(below * below - squared, 0.0)
                / jnp.maximum(4.0 * below * below - 1.0, 1.0)
            ),
            0.0,
        )
        first = degree == order
        current = []
        for t in range(3):
            lanes = pl.ds(t * 128, 128)
            value = alpha * (cosine_ref[:, lanes] * previous[t] - beta * earlier[t]) + jnp.where(
                first, start_ref[:, lanes], 0.0
            )
            rows_ref[t, pl.ds(pl.multiple_of(l * 8, 8), 8), :] = value
            current.append(value)
        return (tuple(current), previous)

    zeros = (jnp.zeros((8, 128), f32),) * 3

    def block(i, carry):
        for u in range(8):
            carry = step(i * 8 + u, carry)
        return carry

    lax.fori_loop(0, 48, block, (zeros, zeros))
    for m3 in range(3):
        for t in range(3):
            parts = [rows_ref[t, pl.ds(r * 8 + m3, 128, stride=24), :] for r in range(3)]
            table = jnp.concatenate(parts, axis=0)
            l_ref[m3, :, pl.ds(t * 128, 128)] = table.astype(bf16)


def legendre_kernel(side, x_ref, l_ref, s_ref, in_ref, out_ref):
    reopen_modes(x_ref, in_ref)
    out_ref[...] = jnp.zeros(out_ref.shape, f32)
    for m3 in range(3):
        halves = [
            jnp.concatenate(
                [in_ref[t, pl.ds(cs * 3 + m3, 128, stride=8), :] for t in range(3)], axis=0
            )
            for cs in range(2)
        ]
        result = lax.dot_general(
            l_ref[m3],
            jnp.concatenate(halves, axis=1).astype(bf16),
            (((side,), (0,)), ((), ())),
            preferred_element_type=f32,
        )
        for t in range(3):
            for cs in range(2):
                out_ref[t, pl.ds(cs * 3 + m3, 128, stride=8), :] = result[
                    t * 128 : (t + 1) * 128, cs * 128 : (cs + 1) * 128
                ]
    close_modes(out_ref, s_ref)


def mix_weight_kernel(w_ref, o_ref, full_ref):
    spread = widen()
    o_ref[...] = jnp.zeros(o_ref.shape, bf16)
    for r in range(3):
        for og in range(3):
            for it in range(3):
                a, i = weight_tile(r, og, it)
                full_ref[:, og, :, pl.ds(it * 128, 128)] = w_ref[a].astype(f32)[
                    :, 8 * i : 8 * i + 8
                ]
        part = full_ref[...].reshape(384, 384).astype(bf16)
        wide = dot(part, spread).astype(bf16)
        for b in range(4):
            o_ref[r, pl.ds(b * 128, 96), :] = wide[b * 96 : (b + 1) * 96]


def mix_kernel(x_ref, w_ref, s_ref, in_ref, out_ref):
    reopen_modes(x_ref, in_ref)
    for r in range(3):
        part = in_ref[r].reshape(32, 4, 8, 128)
        modes = jnp.concatenate([part[:, b].reshape(256, 128) for b in range(4)], axis=1)
        mixed = dot_nt(modes.astype(bf16), w_ref[r])
        back = [mixed[:, b * 128 : (b + 1) * 128].reshape(32, 1, 8, 128) for b in range(4)]
        out_ref[r] = jnp.concatenate(back, axis=1).reshape(1024, 128)
    close_modes(out_ref, s_ref)


def inverse_kernel(g_ref, x_ref, state_ref, s_ref, y_ref, m_ref, h_ref):
    reopen_modes(x_ref, y_ref)
    for parity in range(2):
        for j in range(6):
            first = (parity + j % 3) % 2 * 8 + j
            rows = pl.ds(parity * 384 + j * 64, 64)
            for t in range(3):
                part = y_ref[t, pl.ds(first, 64, stride=16), :]
                m_ref[rows, pl.ds(t * 128, 128)] = part.astype(bf16)
    for block in range(2):
        rows = pl.ds(block * 256, 256)
        even = dot(g_ref[rows, 0:384], m_ref[0:384, :])
        odd = dot(g_ref[rows, 384:768], m_ref[384:768, :])
        for half, spatial in enumerate((even + odd, even - odd)):
            rows = pl.ds(half * 512 + block * 256, 256)
            h_ref[rows, :] = state_ref[rows, :].astype(f32) + jax.nn.gelu(spatial)
    row = iota((8, 128), 0)
    for q in range(16):
        inner, halo = [], []
        for t in range(3):
            lanes = pl.ds(t * 128, 128)
            inner.append(h_ref[pl.ds(q * 64, 64), lanes])
            right = h_ref[pl.ds((q + 1) % 16 * 64, 1), lanes]
            left = h_ref[pl.ds((q * 64 + 1023) % 1024, 1), lanes]
            halo.append(jnp.where(row == 0, right, jnp.where(row == 1, left, 0.0)))
        first, last = close_cells(*inner)
        first_halo, last_halo = close(*halo)
        rest = pltpu.roll(halo[1], 64, 1)
        first_halo = jnp.where(row == 2, pltpu.roll(rest, 2, 0), first_halo)
        last_halo = jnp.where(row == 2, pltpu.roll(rest, 1, 0), last_halo)
        s_ref[q, :, 0:128] = jnp.concatenate([first, first_halo], axis=0).astype(bf16)
        s_ref[q, :, 128:256] = jnp.concatenate([last, last_halo], axis=0).astype(bf16)


def with_sides(inner, halo):
    return jnp.concatenate([inner, halo, pltpu.roll(halo, 6, 0)], axis=0).astype(bf16)


def tail_weights_kernel(u_ref, w_ref, o_ref, c_ref):
    o_ref[...] = jnp.zeros(o_ref.shape, bf16)
    row, col = iota((1024, 256), 0), iota((1024, 256), 1)
    for q in range(4):
        pick = jnp.where(row == 16 * (col % 64) + 4 * (col // 64) + q, 1.0, 0.0).astype(bf16)
        part = dot(u_ref[...], pick).astype(bf16)
        for b in range(4):
            o_ref[pl.ds(b * 128, 96), pl.ds(q * 256, 256)] = part[b * 96 : (b + 1) * 96]
    for p in range(4):
        blocks = []
        for ds in range(3):
            for window in (0, 1, 2, 3, 4, -1):
                dr = window - p
                if -1 <= dr <= 1:
                    blocks.append(w_ref[3 * (dr + 1) + ds].astype(f32))
                else:
                    blocks.append(jnp.zeros((64, 64), f32))
        c_ref[pl.ds(p * 64, 64), :] = jnp.concatenate(blocks, axis=1).astype(bf16)


def fine_kernel(x_ref, u_ref, bias_ref, o_ref, side_ref, h_ref):
    row = iota((8, 128), 0)
    for a in range(4):
        for b in range(4):
            cells = x_ref[a * 4 + b].astype(f32)
            first, last = cells[:, 0:128], cells[:, 128:256]
            first_halo, last_halo = first[72:80], last[72:80]
            rest = jnp.where(
                row == 0,
                pltpu.roll(pltpu.roll(first_halo, 64, 1), 6, 0),
                pltpu.roll(pltpu.roll(last_halo, 64, 1), 7, 0),
            )
            tiles = (
                (first[:64], first_halo),
                (reopen_cells(first, last), reopen(first_halo, last_halo, rest)),
                (last[:64], last_halo),
            )
            for t, (inner, halo) in enumerate(tiles):
                h_ref[pl.ds((a * 3 + t) * 80, 80), pl.ds(b * 128, 128)] = with_sides(inner, halo)
    for q in range(4):
        lanes = pl.ds(q * 256, 256)
        for block in range(4):
            rows = pl.ds(block * 240, 240)
            value = dot(h_ref[rows, :], u_ref[:, lanes]) + bias_ref[:, lanes]
            value = jax.nn.gelu(value).astype(bf16)
            for i in range(3):
                a = block * 3 + i
                o_ref[q, pl.ds(a * 64, 64), :] = value[i * 80 : i * 80 + 64]
                side_ref[q, pl.ds(a * 16, 16), :] = value[i * 80 + 64 : i * 80 + 80]


def conv_kernel(
    ends_ref, f_ref, side_ref, up_ref, down_ref, u_ref, bias_ref, w_ref, cb_ref, o_ref,
    h_ref, e_ref, t_ref, s_ref, z_ref, g_ref,
):
    for b in range(4):
        lanes = pl.ds(b * 128, 128)
        for side, ref in enumerate((up_ref, down_ref)):
            cells = ref[b].astype(f32)
            h_ref[pl.ds(side * 80, 80), lanes] = with_sides(cells[:64], cells[72:80])
    keep = jnp.where(iota((160, 256), 0) < 80, ends_ref[0], ends_ref[1]) > 0

    def around(q, ref, a, size, start):
        half = iota((size, 128), 1) < 64
        below = e_ref[pl.ds(80 + start, size), 0:128]
        above = e_ref[pl.ds(start, size), 128:256]
        if a < 11:
            below = ref[q, pl.ds((a + 1) * size, size), 0:128]
        if a > 0:
            above = ref[q, pl.ds((a - 1) * size, size), 128:256]
        return jnp.where(half, below, above)

    for q in range(4):
        lanes = pl.ds(q * 256, 256)
        value = jax.nn.gelu(dot(h_ref[...], u_ref[:, lanes]) + bias_ref[:, lanes])
        e_ref[...] = jnp.where(keep, value, 0.0).astype(bf16)
        for a in range(12):
            rows = pl.ds(a * 64, 64)
            outer = around(q, f_ref, a, 64, 0)
            t_ref[q, rows, :] = outer
            if q in (0, 3):
                side, amount = (0, 1) if q == 3 else (1, 79)
                edges = pl.ds(a * 16, 16)
                for t in range(3):
                    if t < 2:
                        inner = f_ref[q, rows, t * 128 : (t + 1) * 128]
                        edge = side_ref[q, edges, t * 128 : (t + 1) * 128]
                    else:
                        inner, edge = outer, around(q, side_ref, a, 16, 64)
                    column = jnp.concatenate([inner, edge], axis=0).astype(f32)
                    column = pltpu.roll(column, amount, 0)[:64]
                    s_ref[side, rows, pl.ds(t * 128, 128)] = column.astype(bf16)
    for q in range(4):
        parts = []
        for source in (q - 1, q, q + 1):
            if 0 <= source < 4:
                parts += [f_ref[source], t_ref[source]]
            else:
                parts.append(s_ref[0 if source < 0 else 1])
        total = dot_nt(jnp.concatenate(parts, axis=1), w_ref[...])
        z_ref[q] = (total + f_ref[q].astype(f32) + cb_ref[...]).astype(bf16)
    row, col = iota((256, 256), 0), iota((256, 256), 1)
    place = jnp.where(col == 4 * (row % 64) + row // 64, 1.0, 0.0).astype(bf16)
    for a in range(12):
        cells = jnp.concatenate([z_ref[q, pl.ds(a * 64, 64), :] for q in range(4)], axis=0)
        lines = lax.dot_general(cells, place, (((0,), (0,)), ((), ())), preferred_element_type=f32)
        for p in range(4):
            for t in range(2):
                g_ref[t, pl.ds(4 * a + p, 64, stride=48), :] = lines[
                    p * 64 : (p + 1) * 64, t * 128 : (t + 1) * 128
                ]
    for t in range(2):
        o_ref[:, :, pl.ds(t * 128, 128)] = g_ref[t].reshape(64, 48, 128).astype(bf16)


def start_logs(degrees):
    values = []
    total = 0.0
    for m in range(degrees):
        if m > 0:
            total = total + math.log((2.0 * m - 1.0) / (2.0 * m))
        values.append(0.5 * (math.log((2.0 * m + 1.0) / (4.0 * math.pi)) + total))
    return values


def legendre_tables(n):
    order = 3 * n + jnp.arange(8, dtype=jnp.int32)
    lane = jnp.arange(384, dtype=jnp.int32)
    colatitude = ((3 * (lane % 128) + lane // 128).astype(f32) + 0.5) * (math.pi / 384)
    cosine = jnp.broadcast_to(jnp.cos(colatitude)[None, :], (8, 384))
    log_sine = jnp.log(jnp.sin(colatitude))[None, :]
    logs = jnp.asarray(start_logs(384), f32)
    log_base = jnp.sum(jnp.where(order[:, None] == lane[None, :], logs[None, :], 0.0), axis=1)
    log_start = log_base[:, None] + order.astype(f32)[:, None] * log_sine
    start = jnp.where(log_start > -80.0, jnp.exp(jnp.maximum(log_start, -80.0)), 0.0)
    orders = jnp.broadcast_to(order.astype(f32)[:, None], (8, 128))
    return call(
        legendre_tables_kernel,
        shape((3, 384, 384)),
        orders,
        cosine,
        start,
        scratch=[pltpu.VMEM((3, 3072, 128), f32)],
        flops=4 * 10**9,
    )


def dft_tables():
    step = 2.0 * math.pi / 1024

    def waves(wave, sine, y, scale):
        angle = ((wave * y + 256 * sine) % 1024).astype(f32) * step
        return jnp.cos(angle) * scale, jnp.sin(angle) * scale

    def turns(wave, block):
        turn = (wave * block % 8).astype(f32) * (math.pi / 4)
        return jnp.cos(turn), jnp.sin(turn)

    row = jnp.arange(768, dtype=jnp.int32)[:, None]
    wave, sine = 3 * (row % 128) + row // 128 % 3, row // 384
    forward = (*waves(wave, sine, iota((1, 128), 1), 1.0), *turns(wave, iota((1, 8), 1)))
    col = jnp.arange(768, dtype=jnp.int32)[None, :]
    j = col % 384 // 64
    wave = 3 * (2 * (col % 64) + (col // 384 + j % 3) % 2) + j % 3
    scale = jnp.where(wave == 0, 1.0, 2.0)
    inverse = (*waves(wave, j // 3, iota((128, 1), 0), scale), *turns(wave, iota((8, 1), 0)))
    return call(
        dft_tables_kernel,
        (shape((768, 1024)), shape((512, 768))),
        *forward,
        *inverse,
        flops=4 * 10**9,
    )


def exchange(x, axes):
    return lax.all_to_all(x, axes, 0, 0, tiled=True)


def local(state_field, mix_weight, upsample_weight, upsample_bias, conv_weight, conv_bias):
    lat = lax.axis_index("lat")
    n = 4 * lat + lax.axis_index("qa")
    packed = call(pack_kernel, shape((16, 104, 256)), state_field, mix_weight, flops=10**9)
    arrived = exchange(packed, ("qa", "qb"))
    forward, inverse = dft_tables()
    basis = legendre_tables(n)
    arrived, basis = lax.optimization_barrier((arrived, basis))
    colatitude = ((3 * n + jnp.arange(384, dtype=jnp.int32) // 128).astype(f32) + 0.5) * (
        math.pi / 384
    )
    scale = (jnp.sin(colatitude) * (math.pi / 384) * (2.0 * math.pi / 1024))[None, :]
    scratch = [pltpu.VMEM((3, 1024, 128), f32)] * 2
    spectra, state, own = call(
        dft_kernel,
        (shape((1024, 256)), shape((1024, 384)), shape((16, 56, 128))),
        forward,
        arrived,
        scale,
        scratch=scratch[:1],
        flops=10**9,
    )
    columns = exchange(spectra, ("lat", "qa"))

    def transform(x, side):
        kernel = functools.partial(legendre_kernel, side)
        return call(kernel, shape((1024, 256)), x, basis, scratch=scratch, flops=10**9)

    coeffs = transform(columns, 1)
    spread_up, spread_conv = call(
        tail_weights_kernel,
        (shape((512, 1024)), shape((256, 1152))),
        upsample_weight,
        conv_weight,
        flops=2 * 10**9,
    )
    gathered = lax.all_gather(own, "qa", axis=0)
    coeffs, gathered = lax.optimization_barrier((coeffs, gathered))
    degrees = exchange(coeffs, ("lat", "qb"))
    mixer = call(
        mix_weight_kernel,
        shape((3, 512, 512)),
        gathered,
        scratch=[pltpu.VMEM((16, 3, 8, 384), f32)],
        flops=10**9,
    )
    mixed = call(mix_kernel, shape((1024, 256)), degrees, mixer, scratch=scratch, flops=10**9)
    mixed, spread_up, spread_conv = lax.optimization_barrier((mixed, spread_up, spread_conv))
    returned = exchange(mixed, ("lat", "qb"))
    synthesized = transform(returned, 0)
    modes = exchange(synthesized, ("lat", "qa"))
    hidden = call(
        inverse_kernel,
        shape((16, 80, 256)),
        inverse,
        modes,
        state,
        scratch=[scratch[0], pltpu.VMEM((768, 384), bf16), pltpu.VMEM((1024, 384), f32)],
        flops=10**9,
    )
    cells = exchange(hidden, ("qa", "qb"))
    first_row = cells[0:4, :, 0:128]
    last_row = cells[12:16, :, 128:256]
    count = lax.axis_size("lat")
    up = lax.ppermute(last_row, "lat", [(i, i + 1) for i in range(count - 1)])
    down = lax.ppermute(first_row, "lat", [(i + 1, i) for i in range(count - 1)])
    bias = jnp.tile(upsample_bias, 16)[None, :]
    fine, sides = call(
        fine_kernel,
        (shape((4, 768, 256)), shape((4, 192, 256))),
        cells,
        spread_up,
        bias,
        scratch=[pltpu.VMEM((960, 512), bf16)],
        flops=10**10,
    )
    ends = jnp.stack([lat > 0, lat < count - 1]).astype(jnp.int32)
    return call(
        conv_kernel,
        shape((64, 48, 256)),
        ends,
        fine,
        sides,
        up,
        down,
        spread_up,
        bias,
        spread_conv,
        jnp.tile(conv_bias, 4)[None, :],
        smem=(0,),
        scratch=[
            pltpu.VMEM((160, 512), bf16),
            pltpu.VMEM((160, 256), bf16),
            pltpu.VMEM((4, 768, 128), bf16),
            pltpu.VMEM((2, 768, 384), bf16),
            pltpu.VMEM((4, 768, 256), bf16),
            pltpu.VMEM((2, 3072, 128), f32),
        ],
        flops=10**10,
    )


def solution(mesh):
    fine_mesh = Mesh(mesh.devices.reshape(32, 4, 4), ("lat", "qa", "qb"))
    rows = P("lat", ("qa", "qb"), None)
    return jax.shard_map(
        local,
        mesh=fine_mesh,
        in_specs=(rows, rows, P(), P(), P(), P()),
        out_specs=P(None, "lat", ("qa", "qb")),
        check_vma=False,
    )
```

```python
import functools
import math

import jax
import jax.numpy as jnp
from jax import lax
from jax.experimental import pallas as pl
from jax.experimental.pallas import tpu as pltpu
from jax.sharding import Mesh
from jax.sharding import PartitionSpec as P

f32 = jnp.float32
bf16 = jnp.bfloat16
MIB = 1 << 20


def call(kernel, out, *args, scratch=(), flops=0, smem=(), far=(), vmem=40):
    space = [
        pl.BlockSpec(
            memory_space=pltpu.SMEM if i in smem else pltpu.HBM if i in far else pltpu.VMEM
        )
        for i in range(len(args))
    ]
    outs = out if isinstance(out, (tuple, list)) else (out,)
    moved = sum(x.size * x.dtype.itemsize for x in (*args, *outs))
    return pl.pallas_call(
        kernel,
        out_shape=out,
        in_specs=space,
        out_specs=jax.tree.map(
            lambda _: pl.BlockSpec(memory_space=pltpu.HBM if "out" in far else pltpu.VMEM), out
        ),
        scratch_shapes=list(scratch),
        compiler_params=pltpu.CompilerParams(vmem_limit_bytes=vmem * MIB),
        cost_estimate=pl.CostEstimate(flops=flops, bytes_accessed=moved, transcendentals=0),
    )(*args)


def shape(dims, dtype=bf16):
    return jax.ShapeDtypeStruct(dims, dtype)


def iota(dims, axis):
    return lax.broadcasted_iota(jnp.int32, dims, axis)


def widen():
    row, col = iota((384, 512), 0), iota((384, 512), 1)
    return jnp.where((col % 128 < 96) & (row == col // 128 * 96 + col % 128), 1.0, 0.0).astype(bf16)


def dot(a, b):
    return jnp.dot(a, b, preferred_element_type=f32)


def dot_nt(a, b):
    return lax.dot_general(a, b, (((1,), (1,)), ((), ())), preferred_element_type=f32)


def lanes_of(x):
    return iota(x.shape, 1)


def close(first, middle, last):
    lane = lanes_of(first)
    return (
        jnp.where(lane < 96, first, pltpu.roll(middle, 96, 1)),
        jnp.where(lane < 96, last, pltpu.roll(middle, 64, 1)),
    )


def reopen(first, last, rest):
    lane = lanes_of(first)
    return jnp.where(
        lane < 32, pltpu.roll(first, 32, 1), jnp.where(lane < 64, pltpu.roll(last, 64, 1), rest)
    )


def side_by_side(parts):
    group = lanes_of(parts[0]) // 32
    total = jnp.zeros(parts[0].shape, f32)
    for i, part in enumerate(parts):
        total = jnp.where(group == i, pltpu.roll(part, (32 * i + 64) % 128, 1), total)
    return total


def apart(x, i):
    return pltpu.roll(x, (64 - 32 * i) % 128, 1)


def close_cells(first, middle, last):
    a, b = close(first, middle, last)
    pieces = [middle[8 * g : 8 * g + 8] for g in range(8)]
    return (
        jnp.concatenate([a, side_by_side(pieces[:4])], axis=0),
        jnp.concatenate([b, side_by_side(pieces[4:])], axis=0),
    )


def reopen_cells(first, last):
    rest = [apart(first[64:72], i) for i in range(4)] + [apart(last[64:72], i) for i in range(4)]
    return reopen(first[:64], last[:64], jnp.concatenate(rest, axis=0))


def mode_row(j):
    return pl.ds(j, 128, stride=8)


def close_modes(y_ref, s_ref):
    a, b = close(y_ref[0], y_ref[1], y_ref[2])
    y_ref[0], y_ref[2] = a, b
    y_ref[0, mode_row(6), :] = side_by_side([y_ref[1, mode_row(j), :] for j in range(4)])
    y_ref[2, mode_row(6), :] = side_by_side([y_ref[1, mode_row(j), :] for j in range(4, 6)])
    s_ref[:, 0:128] = y_ref[0].astype(bf16)
    s_ref[:, 128:256] = y_ref[2].astype(bf16)


def reopen_modes(x_ref, y_ref):
    first, last = x_ref[:, 0:128].astype(f32), x_ref[:, 128:256].astype(f32)
    y_ref[0], y_ref[2] = first, last
    y_ref[1] = reopen(first, last, jnp.zeros(first.shape, f32))
    rest = y_ref[0, mode_row(6), :], y_ref[2, mode_row(6), :]
    upper = lanes_of(rest[0]) >= 64
    for j in range(6):
        y_ref[1, mode_row(j), :] = jnp.where(
            upper, apart(rest[j // 4], j % 4), y_ref[1, mode_row(j), :]
        )


def weight_tile(r, og, it):
    index = r * 9 + og * 3 + it
    return index // 7, index % 7


def pack_kernel(x_far, w_far, s_far, x_ref, w_ref, s_ref, in_sems, out_sems):
    arriving = [pltpu.make_async_copy(w_far, w_ref, in_sems.at[4])]
    for a in range(4):
        rows = pl.ds(3 * a, 3)
        arriving.append(pltpu.make_async_copy(x_far.at[rows], x_ref.at[rows], in_sems.at[a]))
    for copy in arriving:
        copy.start()
    arriving[0].wait()
    leaving = []
    spread = widen()
    blank = jnp.zeros((8, 128), f32)
    for a in range(4):
        arriving[a + 1].wait()
        wide = [dot(x_ref[3 * a + t], spread) for t in range(3)]
        for b in range(4):
            first, last = close_cells(*(w[:, b * 128 : (b + 1) * 128] for w in wide))
            tiles = {}
            for r in range(3):
                weights = w_ref[3 * b + r].astype(f32)
                for og in range(3):
                    for it in range(3):
                        tiles[weight_tile(r, og, it)] = weights[
                            8 * og : 8 * og + 8, 128 * it : 128 * it + 128
                        ]
            for side, cells in enumerate((first, last)):
                parts = [tiles.get((a, 2 * row + side), blank) for row in range(4)]
                s_ref[a * 4 + b, :, pl.ds(side * 128, 128)] = jnp.concatenate(
                    [cells, *parts], axis=0
                ).astype(bf16)
        done = pl.ds(a * 4, 4)
        leaving.append(pltpu.make_async_copy(s_ref.at[done], s_far.at[done], out_sems.at[a]))
        leaving[a].start()
    for copy in leaving:
        copy.wait()


def dft_tables_kernel(p_ref, q_ref, cb_ref, sb_ref, pt_ref, qt_ref, cbt_ref, sbt_ref, c_ref, g_ref):
    for b in range(8):
        c_ref[:, pl.ds(b * 128, 128)] = (
            p_ref[...] * cb_ref[:, b : b + 1] - q_ref[...] * sb_ref[:, b : b + 1]
        ).astype(bf16)
    for b in range(4):
        g_ref[pl.ds(b * 128, 128), :] = (
            pt_ref[...] * cbt_ref[b : b + 1, :] - qt_ref[...] * sbt_ref[b : b + 1, :]
        ).astype(bf16)


def dft_kernel(c_ref, x_ref, w_ref, s_ref, state_ref, part_ref, y_ref):
    for q in range(16):
        cells = x_ref[q].astype(f32)
        first, last = cells[:, 0:128], cells[:, 128:256]
        rows = pl.ds(q * 64, 64)
        state_ref[rows, 0:128] = first[:64].astype(bf16)
        state_ref[rows, 128:256] = reopen_cells(first, last).astype(bf16)
        state_ref[rows, 256:384] = last[:64].astype(bf16)
        parts = [
            cells[72 + i // 2 * 8 : 80 + i // 2 * 8, i % 2 * 128 : i % 2 * 128 + 128]
            for i in range(7)
        ]
        part_ref[q] = jnp.concatenate(parts, axis=0).astype(bf16)
    for t in range(3):
        for j in (6, 7):
            y_ref[t, mode_row(j), :] = jnp.zeros((128, 128), f32)
    for block in range(3):
        result = dot(c_ref[pl.ds(block * 256, 256), :], state_ref[...]) * w_ref[...]
        for t in range(3):
            for i in range(2):
                y_ref[t, mode_row(2 * block + i), :] = result[
                    i * 128 : (i + 1) * 128, t * 128 : (t + 1) * 128
                ]
    close_modes(y_ref, s_ref)


def legendre_tables_kernel(order_ref, cosine_ref, start_ref, l_ref, rows_ref):
    order = order_ref[...]
    squared = order * order
    rows_ref[...] = jnp.zeros(rows_ref.shape, f32)

    def step(l, carry):
        previous, earlier = carry
        degree = l.astype(f32)
        above = degree > order
        spacing = jnp.where(above, degree * degree - squared, 1.0)
        alpha = jnp.where(
            above, jnp.sqrt(jnp.maximum(4.0 * degree * degree - 1.0, 1.0) / spacing), 0.0
        )
        below = degree - 1.0
        beta = jnp.where(
            degree > order + 1.0,
            jnp.sqrt(
                jnp.maximum(below * below - squared, 0.0)
                / jnp.maximum(4.0 * below * below - 1.0, 1.0)
            ),
            0.0,
        )
        first = degree == order
        current = []
        for t in range(3):
            lanes = pl.ds(t * 128, 128)
            value = alpha * (cosine_ref[:, lanes] * previous[t] - beta * earlier[t]) + jnp.where(
                first, start_ref[:, lanes], 0.0
            )
            rows_ref[t, pl.ds(pl.multiple_of(l * 8, 8), 8), :] = value
            current.append(value)
        return (tuple(current), previous)

    zeros = (jnp.zeros((8, 128), f32),) * 3

    def block(i, carry):
        for u in range(8):
            carry = step(i * 8 + u, carry)
        return carry

    lax.fori_loop(0, 48, block, (zeros, zeros))
    for m3 in range(3):
        for t in range(3):
            parts = [rows_ref[t, pl.ds(r * 8 + m3, 128, stride=24), :] for r in range(3)]
            table = jnp.concatenate(parts, axis=0)
            l_ref[m3, :, pl.ds(t * 128, 128)] = table.astype(bf16)


def legendre_kernel(side, x_ref, l_ref, s_ref, in_ref, out_ref):
    reopen_modes(x_ref, in_ref)
    out_ref[...] = jnp.zeros(out_ref.shape, f32)
    for m3 in range(3):
        halves = [
            jnp.concatenate(
                [in_ref[t, pl.ds(cs * 3 + m3, 128, stride=8), :] for t in range(3)], axis=0
            )
            for cs in range(2)
        ]
        result = lax.dot_general(
            l_ref[m3],
            jnp.concatenate(halves, axis=1).astype(bf16),
            (((side,), (0,)), ((), ())),
            preferred_element_type=f32,
        )
        for t in range(3):
            for cs in range(2):
                out_ref[t, pl.ds(cs * 3 + m3, 128, stride=8), :] = result[
                    t * 128 : (t + 1) * 128, cs * 128 : (cs + 1) * 128
                ]
    close_modes(out_ref, s_ref)


def mix_weight_kernel(w_ref, o_ref, full_ref):
    spread = widen()
    o_ref[...] = jnp.zeros(o_ref.shape, bf16)
    for r in range(3):
        for og in range(3):
            for it in range(3):
                a, i = weight_tile(r, og, it)
                full_ref[:, og, :, pl.ds(it * 128, 128)] = w_ref[a].astype(f32)[
                    :, 8 * i : 8 * i + 8
                ]
        part = full_ref[...].reshape(384, 384).astype(bf16)
        wide = dot(part, spread).astype(bf16)
        for b in range(4):
            o_ref[r, pl.ds(b * 128, 96), :] = wide[b * 96 : (b + 1) * 96]


def mix_kernel(x_ref, w_ref, s_ref, in_ref, out_ref):
    reopen_modes(x_ref, in_ref)
    for r in range(3):
        part = in_ref[r].reshape(32, 4, 8, 128)
        modes = jnp.concatenate([part[:, b].reshape(256, 128) for b in range(4)], axis=1)
        mixed = dot_nt(modes.astype(bf16), w_ref[r])
        back = [mixed[:, b * 128 : (b + 1) * 128].reshape(32, 1, 8, 128) for b in range(4)]
        out_ref[r] = jnp.concatenate(back, axis=1).reshape(1024, 128)
    close_modes(out_ref, s_ref)


def inverse_kernel(g_ref, x_ref, state_ref, s_ref, y_ref, m_ref, h_ref):
    reopen_modes(x_ref, y_ref)
    for parity in range(2):
        for j in range(6):
            first = (parity + j % 3) % 2 * 8 + j
            rows = pl.ds(parity * 384 + j * 64, 64)
            for t in range(3):
                part = y_ref[t, pl.ds(first, 64, stride=16), :]
                m_ref[rows, pl.ds(t * 128, 128)] = part.astype(bf16)
    for block in range(2):
        rows = pl.ds(block * 256, 256)
        even = dot(g_ref[rows, 0:384], m_ref[0:384, :])
        odd = dot(g_ref[rows, 384:768], m_ref[384:768, :])
        for half, spatial in enumerate((even + odd, even - odd)):
            rows = pl.ds(half * 512 + block * 256, 256)
            h_ref[rows, :] = state_ref[rows, :].astype(f32) + jax.nn.gelu(spatial)
    row = iota((8, 128), 0)
    for q in range(16):
        inner, halo = [], []
        for t in range(3):
            lanes = pl.ds(t * 128, 128)
            inner.append(h_ref[pl.ds(q * 64, 64), lanes])
            right = h_ref[pl.ds((q + 1) % 16 * 64, 1), lanes]
            left = h_ref[pl.ds((q * 64 + 1023) % 1024, 1), lanes]
            halo.append(jnp.where(row == 0, right, jnp.where(row == 1, left, 0.0)))
        first, last = close_cells(*inner)
        first_halo, last_halo = close(*halo)
        rest = pltpu.roll(halo[1], 64, 1)
        first_halo = jnp.where(row == 2, pltpu.roll(rest, 2, 0), first_halo)
        last_halo = jnp.where(row == 2, pltpu.roll(rest, 1, 0), last_halo)
        s_ref[q, :, 0:128] = jnp.concatenate([first, first_halo], axis=0).astype(bf16)
        s_ref[q, :, 128:256] = jnp.concatenate([last, last_halo], axis=0).astype(bf16)


def with_sides(inner, halo):
    return jnp.concatenate([inner, halo, pltpu.roll(halo, 6, 0)], axis=0).astype(bf16)


def tail_weights_kernel(u_ref, w_ref, o_ref, c_ref, y_ref):
    o_ref[...] = jnp.zeros(o_ref.shape, bf16)
    row, col = iota((1024, 256), 0), iota((1024, 256), 1)
    for q in range(4):
        pick = jnp.where(row == 16 * (col % 64) + 4 * (col // 64) + q, 1.0, 0.0).astype(bf16)
        part = dot(u_ref[...], pick).astype(bf16)
        for b in range(4):
            o_ref[pl.ds(b * 128, 96), pl.ds(q * 256, 256)] = part[b * 96 : (b + 1) * 96]
    for p in range(4):
        blocks = []
        for ds in range(3):
            for window in (0, 1, 2, 3, 4, -1):
                dr = window - p
                if -1 <= dr <= 1:
                    blocks.append(w_ref[3 * (dr + 1) + ds].astype(f32))
                else:
                    blocks.append(jnp.zeros((64, 64), f32))
        wide = jnp.concatenate(blocks, axis=1)
        for t in range(9):
            y_ref[t, pl.ds(p, 64, stride=4), :] = wide[:, t * 128 : (t + 1) * 128]
    for t in range(9):
        c_ref[:, pl.ds(t * 128, 128)] = y_ref[t].astype(bf16)
    row, col = iota((256, 256), 0), iota((256, 256), 1)
    same = (row // 4 == col % 64) & (row % 4 == col // 64)
    c_ref[:, 1152:1408] = jnp.where(same, 1.0, 0.0).astype(bf16)


def fine_kernel(x_ref, u_ref, bias_ref, o_ref, side_ref, h_ref):
    row = iota((8, 128), 0)
    for a in range(4):
        for b in range(4):
            cells = x_ref[a * 4 + b].astype(f32)
            first, last = cells[:, 0:128], cells[:, 128:256]
            first_halo, last_halo = first[72:80], last[72:80]
            rest = jnp.where(
                row == 0,
                pltpu.roll(pltpu.roll(first_halo, 64, 1), 6, 0),
                pltpu.roll(pltpu.roll(last_halo, 64, 1), 7, 0),
            )
            tiles = (
                (first[:64], first_halo),
                (reopen_cells(first, last), reopen(first_halo, last_halo, rest)),
                (last[:64], last_halo),
            )
            for t, (inner, halo) in enumerate(tiles):
                h_ref[pl.ds((a * 3 + t) * 80, 80), pl.ds(b * 128, 128)] = with_sides(inner, halo)
    for q in range(4):
        lanes = pl.ds(q * 256, 256)
        for block in range(4):
            rows = pl.ds(block * 240, 240)
            value = dot(h_ref[rows, :], u_ref[:, lanes]) + bias_ref[:, lanes]
            value = jax.nn.gelu(value).astype(bf16)
            for i in range(3):
                a = block * 3 + i
                o_ref[q, pl.ds(a * 64, 64), :] = value[i * 80 : i * 80 + 64]
                side_ref[q, pl.ds(a * 16, 16), :] = value[i * 80 + 64 : i * 80 + 80]


def conv_kernel(
    ends_ref, f_ref, side_ref, up_ref, down_ref, u_ref, bias_ref, w_ref, cb_ref, o_ref,
    h_ref, e_ref, t_ref, s_ref, z_ref, g_ref,
):
    for b in range(4):
        lanes = pl.ds(b * 128, 128)
        for side, ref in enumerate((up_ref, down_ref)):
            cells = ref[b].astype(f32)
            h_ref[pl.ds(side * 80, 80), lanes] = with_sides(cells[:64], cells[72:80])
    keep = jnp.where(iota((160, 256), 0) < 80, ends_ref[0], ends_ref[1]) > 0

    def around(q, ref, a, size, start):
        half = iota((size, 128), 1) < 64
        below = e_ref[pl.ds(80 + start, size), 0:128]
        above = e_ref[pl.ds(start, size), 128:256]
        if a < 11:
            below = ref[q, pl.ds((a + 1) * size, size), 0:128]
        if a > 0:
            above = ref[q, pl.ds((a - 1) * size, size), 128:256]
        return jnp.where(half, below, above)

    for q in range(4):
        lanes = pl.ds(q * 256, 256)
        value = jax.nn.gelu(dot(h_ref[...], u_ref[:, lanes]) + bias_ref[:, lanes])
        e_ref[...] = jnp.where(keep, value, 0.0).astype(bf16)
        for a in range(12):
            rows = pl.ds(a * 64, 64)
            outer = around(q, f_ref, a, 64, 0)
            t_ref[q, rows, :] = outer
            if q in (0, 3):
                side, amount = (0, 1) if q == 3 else (1, 79)
                edges = pl.ds(a * 16, 16)
                for t in range(3):
                    if t < 2:
                        inner = f_ref[q, rows, t * 128 : (t + 1) * 128]
                        edge = side_ref[q, edges, t * 128 : (t + 1) * 128]
                    else:
                        inner, edge = outer, around(q, side_ref, a, 16, 64)
                    column = jnp.concatenate([inner, edge], axis=0).astype(f32)
                    column = pltpu.roll(column, amount, 0)[:64]
                    s_ref[side, rows, pl.ds(t * 128, 128)] = column.astype(bf16)
    for q in range(4):
        parts = []
        for source in (q - 1, q, q + 1):
            if 0 <= source < 4:
                parts += [f_ref[source], t_ref[source]]
            else:
                parts.append(s_ref[0 if source < 0 else 1])
        total = dot_nt(jnp.concatenate([*parts, f_ref[q]], axis=1), w_ref[...])
        z_ref[q] = (total + cb_ref[...]).astype(bf16)
    row, col = iota((256, 256), 0), iota((256, 256), 1)
    place = jnp.where(col == 4 * (row % 64) + row // 64, 1.0, 0.0).astype(bf16)
    low = iota((32, 8, 256), 1) < 4
    for h in range(6):
        pair = []
        for a in (2 * h, 2 * h + 1):
            cells = jnp.concatenate([z_ref[q, pl.ds(a * 64, 64), :] for q in range(4)], axis=0)
            lines = lax.dot_general(
                cells, place, (((0,), (0,)), ((), ())), preferred_element_type=f32
            )
            pair.append(lines.reshape(32, 8, 256))
        turned = [pltpu.roll(lines, 4, 1) for lines in pair]
        first = jnp.where(low, pair[0], turned[1])
        second = jnp.where(low, turned[0], pair[1])
        both = jnp.stack([first, second], axis=1).reshape(64, 8, 256)
        g_ref[:, pl.ds(8 * h, 8), :] = both
    o_ref[...] = g_ref[...].astype(bf16)


def start_logs(degrees):
    values = []
    total = 0.0
    for m in range(degrees):
        if m > 0:
            total = total + math.log((2.0 * m - 1.0) / (2.0 * m))
        values.append(0.5 * (math.log((2.0 * m + 1.0) / (4.0 * math.pi)) + total))
    return values


def legendre_tables(n):
    order = 3 * n + jnp.arange(8, dtype=jnp.int32)
    lane = jnp.arange(384, dtype=jnp.int32)
    colatitude = ((3 * (lane % 128) + lane // 128).astype(f32) + 0.5) * (math.pi / 384)
    cosine = jnp.broadcast_to(jnp.cos(colatitude)[None, :], (8, 384))
    log_sine = jnp.log(jnp.sin(colatitude))[None, :]
    logs = jnp.asarray(start_logs(384), f32)
    log_base = jnp.sum(jnp.where(order[:, None] == lane[None, :], logs[None, :], 0.0), axis=1)
    log_start = log_base[:, None] + order.astype(f32)[:, None] * log_sine
    start = jnp.where(log_start > -80.0, jnp.exp(jnp.maximum(log_start, -80.0)), 0.0)
    orders = jnp.broadcast_to(order.astype(f32)[:, None], (8, 128))
    return call(
        legendre_tables_kernel,
        shape((3, 384, 384)),
        orders,
        cosine,
        start,
        scratch=[pltpu.VMEM((3, 3072, 128), f32)],
        flops=4 * 10**9,
    )


def dft_tables():
    step = 2.0 * math.pi / 1024

    def waves(wave, sine, y, scale):
        angle = ((wave * y + 256 * sine) % 1024).astype(f32) * step
        return jnp.cos(angle) * scale, jnp.sin(angle) * scale

    def turns(wave, block):
        turn = (wave * block % 8).astype(f32) * (math.pi / 4)
        return jnp.cos(turn), jnp.sin(turn)

    row = jnp.arange(768, dtype=jnp.int32)[:, None]
    wave, sine = 3 * (row % 128) + row // 128 % 3, row // 384
    forward = (*waves(wave, sine, iota((1, 128), 1), 1.0), *turns(wave, iota((1, 8), 1)))
    col = jnp.arange(768, dtype=jnp.int32)[None, :]
    j = col % 384 // 64
    wave = 3 * (2 * (col % 64) + (col // 384 + j % 3) % 2) + j % 3
    scale = jnp.where(wave == 0, 1.0, 2.0)
    inverse = (*waves(wave, j // 3, iota((128, 1), 0), scale), *turns(wave, iota((8, 1), 0)))
    return call(
        dft_tables_kernel,
        (shape((768, 1024)), shape((512, 768))),
        *forward,
        *inverse,
        flops=4 * 10**9,
    )


def exchange(x, axes):
    return lax.all_to_all(x, axes, 0, 0, tiled=True)


def local(state_field, mix_weight, upsample_weight, upsample_bias, conv_weight, conv_bias):
    lat = lax.axis_index("lat")
    n = 4 * lat + lax.axis_index("qa")
    packed = call(
        pack_kernel,
        shape((16, 104, 256)),
        state_field,
        mix_weight,
        far=(0, 1, "out"),
        vmem=60,
        scratch=[
            pltpu.VMEM((12, 64, 384), bf16),
            pltpu.VMEM((12, 24, 384), bf16),
            pltpu.VMEM((16, 104, 256), bf16),
            pltpu.SemaphoreType.DMA((5,)),
            pltpu.SemaphoreType.DMA((4,)),
        ],
        flops=10**9,
    )
    arrived = exchange(packed, ("qa", "qb"))
    forward, inverse = dft_tables()
    basis = legendre_tables(n)
    arrived, basis = lax.optimization_barrier((arrived, basis))
    colatitude = ((3 * n + jnp.arange(384, dtype=jnp.int32) // 128).astype(f32) + 0.5) * (
        math.pi / 384
    )
    scale = (jnp.sin(colatitude) * (math.pi / 384) * (2.0 * math.pi / 1024))[None, :]
    scratch = [pltpu.VMEM((3, 1024, 128), f32)] * 2
    spectra, state, own = call(
        dft_kernel,
        (shape((1024, 256)), shape((1024, 384)), shape((16, 56, 128))),
        forward,
        arrived,
        scale,
        scratch=scratch[:1],
        flops=10**9,
    )
    columns = exchange(spectra, ("lat", "qa"))

    def transform(x, side):
        kernel = functools.partial(legendre_kernel, side)
        return call(kernel, shape((1024, 256)), x, basis, scratch=scratch, flops=10**9)

    coeffs = transform(columns, 1)
    spread_up, spread_conv = call(
        tail_weights_kernel,
        (shape((512, 1024)), shape((256, 1408))),
        upsample_weight,
        conv_weight,
        scratch=[pltpu.VMEM((9, 256, 128), f32)],
        flops=2 * 10**9,
    )
    gathered = lax.all_gather(own, "qa", axis=0)
    coeffs, gathered = lax.optimization_barrier((coeffs, gathered))
    degrees = exchange(coeffs, ("lat", "qb"))
    mixer = call(
        mix_weight_kernel,
        shape((3, 512, 512)),
        gathered,
        scratch=[pltpu.VMEM((16, 3, 8, 384), f32)],
        flops=10**9,
    )
    mixed = call(mix_kernel, shape((1024, 256)), degrees, mixer, scratch=scratch, flops=10**9)
    mixed, spread_up, spread_conv = lax.optimization_barrier((mixed, spread_up, spread_conv))
    returned = exchange(mixed, ("lat", "qb"))
    synthesized = transform(returned, 0)
    modes = exchange(synthesized, ("lat", "qa"))
    hidden = call(
        inverse_kernel,
        shape((16, 80, 256)),
        inverse,
        modes,
        state,
        scratch=[scratch[0], pltpu.VMEM((768, 384), bf16), pltpu.VMEM((1024, 384), f32)],
        flops=10**9,
    )
    cells = exchange(hidden, ("qa", "qb"))
    first_row = cells[0:4, :, 0:128]
    last_row = cells[12:16, :, 128:256]
    count = lax.axis_size("lat")
    up = lax.ppermute(last_row, "lat", [(i, i + 1) for i in range(count - 1)])
    down = lax.ppermute(first_row, "lat", [(i + 1, i) for i in range(count - 1)])
    bias = jnp.tile(upsample_bias, 16)[None, :]
    fine, sides = call(
        fine_kernel,
        (shape((4, 768, 256)), shape((4, 192, 256))),
        cells,
        spread_up,
        bias,
        scratch=[pltpu.VMEM((960, 512), bf16)],
        flops=10**10,
    )
    ends = jnp.stack([lat > 0, lat < count - 1]).astype(jnp.int32)
    return call(
        conv_kernel,
        shape((64, 48, 256)),
        ends,
        fine,
        sides,
        up,
        down,
        spread_up,
        bias,
        spread_conv,
        jnp.repeat(conv_bias, 4)[None, :],
        smem=(0,),
        scratch=[
            pltpu.VMEM((160, 512), bf16),
            pltpu.VMEM((160, 256), bf16),
            pltpu.VMEM((4, 768, 128), bf16),
            pltpu.VMEM((2, 768, 384), bf16),
            pltpu.VMEM((4, 768, 256), bf16),
            pltpu.VMEM((64, 48, 256), f32),
        ],
        flops=10**10,
    )


def solution(mesh):
    fine_mesh = Mesh(mesh.devices.reshape(32, 4, 4), ("lat", "qa", "qb"))
    rows = P("lat", ("qa", "qb"), None)
    return jax.shard_map(
        local,
        mesh=fine_mesh,
        in_specs=(rows, rows, P(), P(), P(), P()),
        out_specs=P(None, "lat", ("qa", "qb")),
        check_vma=False,
    )
```

```python
import functools
import math

import jax
import jax.numpy as jnp
from jax import lax
from jax.experimental import pallas as pl
from jax.experimental.pallas import tpu as pltpu
from jax.sharding import Mesh
from jax.sharding import PartitionSpec as P

f32 = jnp.float32
bf16 = jnp.bfloat16
MIB = 1 << 20


def call(kernel, out, *args, scratch=(), flops=0, smem=(), far=(), vmem=40):
    space = [
        pl.BlockSpec(
            memory_space=pltpu.SMEM if i in smem else pltpu.HBM if i in far else pltpu.VMEM
        )
        for i in range(len(args))
    ]
    outs = out if isinstance(out, (tuple, list)) else (out,)
    moved = sum(x.size * x.dtype.itemsize for x in (*args, *outs))
    return pl.pallas_call(
        kernel,
        out_shape=out,
        in_specs=space,
        out_specs=jax.tree.map(
            lambda _: pl.BlockSpec(memory_space=pltpu.HBM if "out" in far else pltpu.VMEM), out
        ),
        scratch_shapes=list(scratch),
        compiler_params=pltpu.CompilerParams(vmem_limit_bytes=vmem * MIB),
        cost_estimate=pl.CostEstimate(flops=flops, bytes_accessed=moved, transcendentals=0),
    )(*args)


def shape(dims, dtype=bf16):
    return jax.ShapeDtypeStruct(dims, dtype)


def iota(dims, axis):
    return lax.broadcasted_iota(jnp.int32, dims, axis)


def widen():
    row, col = iota((384, 512), 0), iota((384, 512), 1)
    return jnp.where((col % 128 < 96) & (row == col // 128 * 96 + col % 128), 1.0, 0.0).astype(bf16)


def dot(a, b):
    return jnp.dot(a, b, preferred_element_type=f32)


def dot_nt(a, b):
    return lax.dot_general(a, b, (((1,), (1,)), ((), ())), preferred_element_type=f32)


def lanes_of(x):
    return iota(x.shape, 1)


def close(first, middle, last):
    lane = lanes_of(first)
    return (
        jnp.where(lane < 96, first, pltpu.roll(middle, 96, 1)),
        jnp.where(lane < 96, last, pltpu.roll(middle, 64, 1)),
    )


def reopen(first, last, rest):
    lane = lanes_of(first)
    return jnp.where(
        lane < 32, pltpu.roll(first, 32, 1), jnp.where(lane < 64, pltpu.roll(last, 64, 1), rest)
    )


def side_by_side(parts):
    group = lanes_of(parts[0]) // 32
    total = jnp.zeros(parts[0].shape, f32)
    for i, part in enumerate(parts):
        total = jnp.where(group == i, pltpu.roll(part, (32 * i + 64) % 128, 1), total)
    return total


def apart(x, i):
    return pltpu.roll(x, (64 - 32 * i) % 128, 1)


def close_cells(first, middle, last):
    a, b = close(first, middle, last)
    pieces = [middle[8 * g : 8 * g + 8] for g in range(8)]
    return (
        jnp.concatenate([a, side_by_side(pieces[:4])], axis=0),
        jnp.concatenate([b, side_by_side(pieces[4:])], axis=0),
    )


def reopen_cells(first, last):
    rest = [apart(first[64:72], i) for i in range(4)] + [apart(last[64:72], i) for i in range(4)]
    return reopen(first[:64], last[:64], jnp.concatenate(rest, axis=0))


def mode_row(j):
    return pl.ds(j, 128, stride=8)


def close_modes(y_ref, s_ref):
    a, b = close(y_ref[0], y_ref[1], y_ref[2])
    y_ref[0], y_ref[2] = a, b
    y_ref[0, mode_row(6), :] = side_by_side([y_ref[1, mode_row(j), :] for j in range(4)])
    y_ref[2, mode_row(6), :] = side_by_side([y_ref[1, mode_row(j), :] for j in range(4, 6)])
    s_ref[:, 0:128] = y_ref[0].astype(bf16)
    s_ref[:, 128:256] = y_ref[2].astype(bf16)


def reopen_modes(x_ref, y_ref):
    first, last = x_ref[:, 0:128].astype(f32), x_ref[:, 128:256].astype(f32)
    y_ref[0], y_ref[2] = first, last
    y_ref[1] = reopen(first, last, jnp.zeros(first.shape, f32))
    rest = y_ref[0, mode_row(6), :], y_ref[2, mode_row(6), :]
    upper = lanes_of(rest[0]) >= 64
    for j in range(6):
        y_ref[1, mode_row(j), :] = jnp.where(
            upper, apart(rest[j // 4], j % 4), y_ref[1, mode_row(j), :]
        )


def weight_tile(r, og, it):
    index = r * 9 + og * 3 + it
    return index // 7, index % 7


def pack_kernel(x_far, w_far, s_far, x_ref, w_ref, s_ref, in_sems, out_sems):
    arriving = [pltpu.make_async_copy(w_far, w_ref, in_sems.at[4])]
    for a in range(4):
        rows = pl.ds(3 * a, 3)
        arriving.append(pltpu.make_async_copy(x_far.at[rows], x_ref.at[rows], in_sems.at[a]))
    for copy in arriving:
        copy.start()
    arriving[0].wait()
    leaving = []
    spread = widen()
    blank = jnp.zeros((8, 128), f32)
    for a in range(4):
        arriving[a + 1].wait()
        wide = [dot(x_ref[3 * a + t], spread) for t in range(3)]
        for b in range(4):
            first, last = close_cells(*(w[:, b * 128 : (b + 1) * 128] for w in wide))
            tiles = {}
            for r in range(3):
                weights = w_ref[3 * b + r].astype(f32)
                for og in range(3):
                    for it in range(3):
                        tiles[weight_tile(r, og, it)] = weights[
                            8 * og : 8 * og + 8, 128 * it : 128 * it + 128
                        ]
            parts = [tiles.get((a, i), blank) for i in range(7)]
            s_ref[a * 4 + b] = jnp.concatenate([first, last, *parts], axis=0).astype(bf16)
        done = pl.ds(a * 4, 4)
        leaving.append(pltpu.make_async_copy(s_ref.at[done], s_far.at[done], out_sems.at[a]))
        leaving[a].start()
    for copy in leaving:
        copy.wait()


def dft_tables_kernel(p_ref, q_ref, cb_ref, sb_ref, pt_ref, qt_ref, cbt_ref, sbt_ref, c_ref, g_ref):
    for b in range(8):
        c_ref[:, pl.ds(b * 128, 128)] = (
            p_ref[...] * cb_ref[:, b : b + 1] - q_ref[...] * sb_ref[:, b : b + 1]
        ).astype(bf16)
    for b in range(4):
        g_ref[pl.ds(b * 128, 128), :] = (
            pt_ref[...] * cbt_ref[b : b + 1, :] - qt_ref[...] * sbt_ref[b : b + 1, :]
        ).astype(bf16)


def dft_kernel(c_ref, x_ref, w_ref, s_ref, state_ref, *rest):
    *part_refs, y_ref = rest
    for q in range(16):
        cells = x_ref[q].astype(f32)
        first, last = cells[0:72], cells[72:144]
        rows = pl.ds(q * 64, 64)
        state_ref[rows, 0:128] = first[:64].astype(bf16)
        state_ref[rows, 128:256] = reopen_cells(first, last).astype(bf16)
        state_ref[rows, 256:384] = last[:64].astype(bf16)
        for part, ref in enumerate(part_refs):
            ref[q] = cells[144 + 32 * part : min(176 + 32 * part, 200)].astype(bf16)
    for t in range(3):
        for j in (6, 7):
            y_ref[t, mode_row(j), :] = jnp.zeros((128, 128), f32)
    for block in range(3):
        result = dot(c_ref[pl.ds(block * 256, 256), :], state_ref[...]) * w_ref[...]
        for t in range(3):
            for i in range(2):
                y_ref[t, mode_row(2 * block + i), :] = result[
                    i * 128 : (i + 1) * 128, t * 128 : (t + 1) * 128
                ]
    close_modes(y_ref, s_ref)


def legendre_tables_kernel(order_ref, cosine_ref, start_ref, l_ref, rows_ref):
    order = order_ref[...]
    squared = order * order
    rows_ref[...] = jnp.zeros(rows_ref.shape, f32)

    def step(l, carry):
        previous, earlier = carry
        degree = l.astype(f32)
        above = degree > order
        spacing = jnp.where(above, degree * degree - squared, 1.0)
        alpha = jnp.where(
            above, jnp.sqrt(jnp.maximum(4.0 * degree * degree - 1.0, 1.0) / spacing), 0.0
        )
        below = degree - 1.0
        beta = jnp.where(
            degree > order + 1.0,
            jnp.sqrt(
                jnp.maximum(below * below - squared, 0.0)
                / jnp.maximum(4.0 * below * below - 1.0, 1.0)
            ),
            0.0,
        )
        first = degree == order
        current = []
        for t in range(3):
            lanes = pl.ds(t * 128, 128)
            value = alpha * (cosine_ref[:, lanes] * previous[t] - beta * earlier[t]) + jnp.where(
                first, start_ref[:, lanes], 0.0
            )
            rows_ref[t, pl.ds(pl.multiple_of(l * 8, 8), 8), :] = value
            current.append(value)
        return (tuple(current), previous)

    zeros = (jnp.zeros((8, 128), f32),) * 3

    def block(i, carry):
        for u in range(8):
            carry = step(i * 8 + u, carry)
        return carry

    lax.fori_loop(0, 48, block, (zeros, zeros))
    for m3 in range(3):
        for t in range(3):
            parts = [rows_ref[t, pl.ds(r * 8 + m3, 128, stride=24), :] for r in range(3)]
            table = jnp.concatenate(parts, axis=0)
            l_ref[m3, :, pl.ds(t * 128, 128)] = table.astype(bf16)


def legendre_kernel(side, x_ref, l_ref, s_ref, in_ref, out_ref):
    reopen_modes(x_ref, in_ref)
    out_ref[...] = jnp.zeros(out_ref.shape, f32)
    for m3 in range(3):
        halves = [
            jnp.concatenate(
                [in_ref[t, pl.ds(cs * 3 + m3, 128, stride=8), :] for t in range(3)], axis=0
            )
            for cs in range(2)
        ]
        result = lax.dot_general(
            l_ref[m3],
            jnp.concatenate(halves, axis=1).astype(bf16),
            (((side,), (0,)), ((), ())),
            preferred_element_type=f32,
        )
        for t in range(3):
            for cs in range(2):
                out_ref[t, pl.ds(cs * 3 + m3, 128, stride=8), :] = result[
                    t * 128 : (t + 1) * 128, cs * 128 : (cs + 1) * 128
                ]
    close_modes(out_ref, s_ref)


def mix_weight_kernel(w_ref, v_ref, o_ref, full_ref):
    spread = widen()
    o_ref[...] = jnp.zeros(o_ref.shape, bf16)
    for r in range(3):
        for og in range(3):
            for it in range(3):
                a, i = weight_tile(r, og, it)
                part = (w_ref, v_ref)[i // 4][a].astype(f32)
                full_ref[:, og, :, pl.ds(it * 128, 128)] = part[:, i % 4 * 8 : i % 4 * 8 + 8]
        part = full_ref[...].reshape(384, 384).astype(bf16)
        wide = dot(part, spread).astype(bf16)
        for b in range(4):
            o_ref[r, pl.ds(b * 128, 96), :] = wide[b * 96 : (b + 1) * 96]


def mix_kernel(x_ref, w_ref, s_ref, in_ref, out_ref):
    reopen_modes(x_ref, in_ref)
    for r in range(3):
        part = in_ref[r].reshape(32, 4, 8, 128)
        modes = jnp.concatenate([part[:, b].reshape(256, 128) for b in range(4)], axis=1)
        mixed = dot_nt(modes.astype(bf16), w_ref[r])
        back = [mixed[:, b * 128 : (b + 1) * 128].reshape(32, 1, 8, 128) for b in range(4)]
        out_ref[r] = jnp.concatenate(back, axis=1).reshape(1024, 128)
    close_modes(out_ref, s_ref)


def inverse_kernel(g_ref, x_ref, state_ref, s_ref, y_ref, m_ref, h_ref):
    reopen_modes(x_ref, y_ref)
    for parity in range(2):
        for j in range(6):
            first = (parity + j % 3) % 2 * 8 + j
            rows = pl.ds(parity * 384 + j * 64, 64)
            for t in range(3):
                part = y_ref[t, pl.ds(first, 64, stride=16), :]
                m_ref[rows, pl.ds(t * 128, 128)] = part.astype(bf16)
    for block in range(2):
        rows = pl.ds(block * 256, 256)
        even = dot(g_ref[rows, 0:384], m_ref[0:384, :])
        odd = dot(g_ref[rows, 384:768], m_ref[384:768, :])
        for half, spatial in enumerate((even + odd, even - odd)):
            rows = pl.ds(half * 512 + block * 256, 256)
            h_ref[rows, :] = state_ref[rows, :].astype(f32) + jax.nn.gelu(spatial)
    row = iota((8, 128), 0)
    for q in range(16):
        inner, halo = [], []
        for t in range(3):
            lanes = pl.ds(t * 128, 128)
            inner.append(h_ref[pl.ds(q * 64, 64), lanes])
            right = h_ref[pl.ds((q + 1) % 16 * 64, 1), lanes]
            left = h_ref[pl.ds((q * 64 + 1023) % 1024, 1), lanes]
            halo.append(jnp.where(row == 0, right, jnp.where(row == 1, left, 0.0)))
        first, last = close_cells(*inner)
        first_halo, last_halo = close(*halo)
        rest = pltpu.roll(halo[1], 64, 1)
        first_halo = jnp.where(row == 2, pltpu.roll(rest, 2, 0), first_halo)
        last_halo = jnp.where(row == 2, pltpu.roll(rest, 1, 0), last_halo)
        s_ref[q, :, 0:128] = jnp.concatenate([first, first_halo], axis=0).astype(bf16)
        s_ref[q, :, 128:256] = jnp.concatenate([last, last_halo], axis=0).astype(bf16)


def with_sides(inner, halo):
    return jnp.concatenate([inner, halo, pltpu.roll(halo, 6, 0)], axis=0).astype(bf16)


def tail_weights_kernel(u_ref, w_ref, o_ref, c_ref, y_ref):
    o_ref[...] = jnp.zeros(o_ref.shape, bf16)
    row, col = iota((1024, 256), 0), iota((1024, 256), 1)
    for q in range(4):
        pick = jnp.where(row == 16 * (col % 64) + 4 * (col // 64) + q, 1.0, 0.0).astype(bf16)
        part = dot(u_ref[...], pick).astype(bf16)
        for b in range(4):
            o_ref[pl.ds(b * 128, 96), pl.ds(q * 256, 256)] = part[b * 96 : (b + 1) * 96]
    for p in range(4):
        blocks = []
        for ds in range(3):
            for window in (0, 1, 2, 3, 4, -1):
                dr = window - p
                if -1 <= dr <= 1:
                    blocks.append(w_ref[3 * (dr + 1) + ds].astype(f32))
                else:
                    blocks.append(jnp.zeros((64, 64), f32))
        wide = jnp.concatenate(blocks, axis=1)
        for t in range(9):
            y_ref[t, pl.ds(p, 64, stride=4), :] = wide[:, t * 128 : (t + 1) * 128]
    for t in range(9):
        c_ref[:, pl.ds(t * 128, 128)] = y_ref[t].astype(bf16)
    row, col = iota((256, 256), 0), iota((256, 256), 1)
    same = (row // 4 == col % 64) & (row % 4 == col // 64)
    c_ref[:, 1152:1408] = jnp.where(same, 1.0, 0.0).astype(bf16)


def fine_kernel(x_ref, u_ref, bias_ref, o_ref, side_ref, h_ref):
    row = iota((8, 128), 0)
    for a in range(4):
        for b in range(4):
            cells = x_ref[a * 4 + b].astype(f32)
            first, last = cells[:, 0:128], cells[:, 128:256]
            first_halo, last_halo = first[72:80], last[72:80]
            rest = jnp.where(
                row == 0,
                pltpu.roll(pltpu.roll(first_halo, 64, 1), 6, 0),
                pltpu.roll(pltpu.roll(last_halo, 64, 1), 7, 0),
            )
            tiles = (
                (first[:64], first_halo),
                (reopen_cells(first, last), reopen(first_halo, last_halo, rest)),
                (last[:64], last_halo),
            )
            for t, (inner, halo) in enumerate(tiles):
                h_ref[pl.ds((a * 3 + t) * 80, 80), pl.ds(b * 128, 128)] = with_sides(inner, halo)
    for q in range(4):
        lanes = pl.ds(q * 256, 256)
        for block in range(4):
            rows = pl.ds(block * 240, 240)
            value = dot(h_ref[rows, :], u_ref[:, lanes]) + bias_ref[:, lanes]
            value = jax.nn.gelu(value).astype(bf16)
            for i in range(3):
                a = block * 3 + i
                o_ref[q, pl.ds(a * 64, 64), :] = value[i * 80 : i * 80 + 64]
                side_ref[q, pl.ds(a * 16, 16), :] = value[i * 80 + 64 : i * 80 + 80]


def conv_kernel(
    ends_ref, f_ref, side_ref, up_ref, down_ref, u_ref, bias_ref, w_ref, cb_ref, o_ref,
    h_ref, e_ref, t_ref, s_ref, z_ref, g_ref,
):
    for b in range(4):
        lanes = pl.ds(b * 128, 128)
        for side, ref in enumerate((up_ref, down_ref)):
            cells = ref[b].astype(f32)
            h_ref[pl.ds(side * 80, 80), lanes] = with_sides(cells[:64], cells[72:80])
    keep = jnp.where(iota((160, 256), 0) < 80, ends_ref[0], ends_ref[1]) > 0

    def around(q, ref, a, size, start):
        half = iota((size, 128), 1) < 64
        below = e_ref[pl.ds(80 + start, size), 0:128]
        above = e_ref[pl.ds(start, size), 128:256]
        if a < 11:
            below = ref[q, pl.ds((a + 1) * size, size), 0:128]
        if a > 0:
            above = ref[q, pl.ds((a - 1) * size, size), 128:256]
        return jnp.where(half, below, above)

    for q in range(4):
        lanes = pl.ds(q * 256, 256)
        value = jax.nn.gelu(dot(h_ref[...], u_ref[:, lanes]) + bias_ref[:, lanes])
        e_ref[...] = jnp.where(keep, value, 0.0).astype(bf16)
        for a in range(12):
            rows = pl.ds(a * 64, 64)
            outer = around(q, f_ref, a, 64, 0)
            t_ref[q, rows, :] = outer
            if q in (0, 3):
                side, amount = (0, 1) if q == 3 else (1, 79)
                edges = pl.ds(a * 16, 16)
                for t in range(3):
                    if t < 2:
                        inner = f_ref[q, rows, t * 128 : (t + 1) * 128]
                        edge = side_ref[q, edges, t * 128 : (t + 1) * 128]
                    else:
                        inner, edge = outer, around(q, side_ref, a, 16, 64)
                    column = jnp.concatenate([inner, edge], axis=0).astype(f32)
                    column = pltpu.roll(column, amount, 0)[:64]
                    s_ref[side, rows, pl.ds(t * 128, 128)] = column.astype(bf16)
    for q in range(4):
        parts = []
        for source in (q - 1, q, q + 1):
            if 0 <= source < 4:
                parts += [f_ref[source], t_ref[source]]
            else:
                parts.append(s_ref[0 if source < 0 else 1])
        total = dot_nt(jnp.concatenate([*parts, f_ref[q]], axis=1), w_ref[...])
        z_ref[q] = (total + cb_ref[...]).astype(bf16)
    row, col = iota((256, 256), 0), iota((256, 256), 1)
    place = jnp.where(col == 4 * (row % 64) + row // 64, 1.0, 0.0).astype(bf16)
    low = iota((32, 8, 256), 1) < 4
    for h in range(6):
        pair = []
        for a in (2 * h, 2 * h + 1):
            cells = jnp.concatenate([z_ref[q, pl.ds(a * 64, 64), :] for q in range(4)], axis=0)
            lines = lax.dot_general(
                cells, place, (((0,), (0,)), ((), ())), preferred_element_type=f32
            )
            pair.append(lines.reshape(32, 8, 256))
        turned = [pltpu.roll(lines, 4, 1) for lines in pair]
        first = jnp.where(low, pair[0], turned[1])
        second = jnp.where(low, turned[0], pair[1])
        both = jnp.stack([first, second], axis=1).reshape(64, 8, 256)
        g_ref[:, pl.ds(8 * h, 8), :] = both
    o_ref[...] = g_ref[...].astype(bf16)


def start_logs(degrees):
    values = []
    total = 0.0
    for m in range(degrees):
        if m > 0:
            total = total + math.log((2.0 * m - 1.0) / (2.0 * m))
        values.append(0.5 * (math.log((2.0 * m + 1.0) / (4.0 * math.pi)) + total))
    return values


def legendre_tables(n):
    order = 3 * n + jnp.arange(8, dtype=jnp.int32)
    lane = jnp.arange(384, dtype=jnp.int32)
    colatitude = ((3 * (lane % 128) + lane // 128).astype(f32) + 0.5) * (math.pi / 384)
    cosine = jnp.broadcast_to(jnp.cos(colatitude)[None, :], (8, 384))
    log_sine = jnp.log(jnp.sin(colatitude))[None, :]
    logs = jnp.asarray(start_logs(384), f32)
    log_base = jnp.sum(jnp.where(order[:, None] == lane[None, :], logs[None, :], 0.0), axis=1)
    log_start = log_base[:, None] + order.astype(f32)[:, None] * log_sine
    start = jnp.where(log_start > -80.0, jnp.exp(jnp.maximum(log_start, -80.0)), 0.0)
    orders = jnp.broadcast_to(order.astype(f32)[:, None], (8, 128))
    return call(
        legendre_tables_kernel,
        shape((3, 384, 384)),
        orders,
        cosine,
        start,
        scratch=[pltpu.VMEM((3, 3072, 128), f32)],
        flops=4 * 10**9,
    )


def dft_tables():
    step = 2.0 * math.pi / 1024

    def waves(wave, sine, y, scale):
        angle = ((wave * y + 256 * sine) % 1024).astype(f32) * step
        return jnp.cos(angle) * scale, jnp.sin(angle) * scale

    def turns(wave, block):
        turn = (wave * block % 8).astype(f32) * (math.pi / 4)
        return jnp.cos(turn), jnp.sin(turn)

    row = jnp.arange(768, dtype=jnp.int32)[:, None]
    wave, sine = 3 * (row % 128) + row // 128 % 3, row // 384
    forward = (*waves(wave, sine, iota((1, 128), 1), 1.0), *turns(wave, iota((1, 8), 1)))
    col = jnp.arange(768, dtype=jnp.int32)[None, :]
    j = col % 384 // 64
    wave = 3 * (2 * (col % 64) + (col // 384 + j % 3) % 2) + j % 3
    scale = jnp.where(wave == 0, 1.0, 2.0)
    inverse = (*waves(wave, j // 3, iota((128, 1), 0), scale), *turns(wave, iota((8, 1), 0)))
    return call(
        dft_tables_kernel,
        (shape((768, 1024)), shape((512, 768))),
        *forward,
        *inverse,
        flops=4 * 10**9,
    )


def exchange(x, axes):
    return lax.all_to_all(x, axes, 0, 0, tiled=True)


def local(state_field, mix_weight, upsample_weight, upsample_bias, conv_weight, conv_bias):
    lat = lax.axis_index("lat")
    n = 4 * lat + lax.axis_index("qa")
    packed = call(
        pack_kernel,
        shape((16, 200, 128)),
        state_field,
        mix_weight,
        far=(0, 1, "out"),
        vmem=60,
        scratch=[
            pltpu.VMEM((12, 64, 384), bf16),
            pltpu.VMEM((12, 24, 384), bf16),
            pltpu.VMEM((16, 200, 128), bf16),
            pltpu.SemaphoreType.DMA((5,)),
            pltpu.SemaphoreType.DMA((4,)),
        ],
        flops=10**9,
    )
    arrived = exchange(packed, ("qa", "qb"))
    forward, inverse = dft_tables()
    basis = legendre_tables(n)
    arrived, basis = lax.optimization_barrier((arrived, basis))
    colatitude = ((3 * n + jnp.arange(384, dtype=jnp.int32) // 128).astype(f32) + 0.5) * (
        math.pi / 384
    )
    scale = (jnp.sin(colatitude) * (math.pi / 384) * (2.0 * math.pi / 1024))[None, :]
    scratch = [pltpu.VMEM((3, 1024, 128), f32)] * 2
    spectra, state, *own = call(
        dft_kernel,
        (shape((1024, 256)), shape((1024, 384)), shape((16, 32, 128)), shape((16, 24, 128))),
        forward,
        arrived,
        scale,
        scratch=scratch[:1],
        flops=10**9,
    )
    columns = exchange(spectra, ("lat", "qa"))

    def transform(x, side):
        kernel = functools.partial(legendre_kernel, side)
        return call(kernel, shape((1024, 256)), x, basis, scratch=scratch, flops=10**9)

    coeffs = transform(columns, 1)
    spread_up, spread_conv = call(
        tail_weights_kernel,
        (shape((512, 1024)), shape((256, 1408))),
        upsample_weight,
        conv_weight,
        scratch=[pltpu.VMEM((9, 256, 128), f32)],
        flops=2 * 10**9,
    )
    gathered = lax.all_gather(own[0], "qa", axis=0)
    coeffs, gathered, rest = lax.optimization_barrier((coeffs, gathered, own[1]))
    degrees = exchange(coeffs, ("lat", "qb"))
    mixer = call(
        mix_weight_kernel,
        shape((3, 512, 512)),
        gathered,
        lax.all_gather(rest, "qa", axis=0),
        scratch=[pltpu.VMEM((16, 3, 8, 384), f32)],
        flops=10**9,
    )
    mixed = call(mix_kernel, shape((1024, 256)), degrees, mixer, scratch=scratch, flops=10**9)
    mixed, spread_up, spread_conv = lax.optimization_barrier((mixed, spread_up, spread_conv))
    returned = exchange(mixed, ("lat", "qb"))
    synthesized = transform(returned, 0)
    modes = exchange(synthesized, ("lat", "qa"))
    hidden = call(
        inverse_kernel,
        shape((16, 80, 256)),
        inverse,
        modes,
        state,
        scratch=[scratch[0], pltpu.VMEM((768, 384), bf16), pltpu.VMEM((1024, 384), f32)],
        flops=10**9,
    )
    cells = exchange(hidden, ("qa", "qb"))
    first_row = cells[0:4, :, 0:128]
    last_row = cells[12:16, :, 128:256]
    count = lax.axis_size("lat")
    up = lax.ppermute(last_row, "lat", [(i, i + 1) for i in range(count - 1)])
    down = lax.ppermute(first_row, "lat", [(i + 1, i) for i in range(count - 1)])
    bias = jnp.tile(upsample_bias, 16)[None, :]
    fine, sides = call(
        fine_kernel,
        (shape((4, 768, 256)), shape((4, 192, 256))),
        cells,
        spread_up,
        bias,
        scratch=[pltpu.VMEM((960, 512), bf16)],
        flops=10**10,
    )
    ends = jnp.stack([lat > 0, lat < count - 1]).astype(jnp.int32)
    return call(
        conv_kernel,
        shape((64, 48, 256)),
        ends,
        fine,
        sides,
        up,
        down,
        spread_up,
        bias,
        spread_conv,
        jnp.repeat(conv_bias, 4)[None, :],
        smem=(0,),
        scratch=[
            pltpu.VMEM((160, 512), bf16),
            pltpu.VMEM((160, 256), bf16),
            pltpu.VMEM((4, 768, 128), bf16),
            pltpu.VMEM((2, 768, 384), bf16),
            pltpu.VMEM((4, 768, 256), bf16),
            pltpu.VMEM((64, 48, 256), f32),
        ],
        flops=10**10,
    )


def solution(mesh):
    fine_mesh = Mesh(mesh.devices.reshape(32, 4, 4), ("lat", "qa", "qb"))
    rows = P("lat", ("qa", "qb"), None)
    return jax.shard_map(
        local,
        mesh=fine_mesh,
        in_specs=(rows, rows, P(), P(), P(), P()),
        out_specs=P(None, "lat", ("qa", "qb")),
        check_vma=False,
    )
```

```python
import functools
import math

import jax
import jax.numpy as jnp
from jax import lax
from jax.experimental import pallas as pl
from jax.experimental.pallas import tpu as pltpu
from jax.sharding import Mesh
from jax.sharding import PartitionSpec as P

f32 = jnp.float32
bf16 = jnp.bfloat16
MIB = 1 << 20


def call(kernel, out, *args, scratch=(), flops=0, smem=(), far=(), vmem=40):
    space = [
        pl.BlockSpec(
            memory_space=pltpu.SMEM if i in smem else pltpu.HBM if i in far else pltpu.VMEM
        )
        for i in range(len(args))
    ]
    outs = out if isinstance(out, (tuple, list)) else (out,)
    moved = sum(x.size * x.dtype.itemsize for x in (*args, *outs))
    return pl.pallas_call(
        kernel,
        out_shape=out,
        in_specs=space,
        out_specs=jax.tree.map(
            lambda _: pl.BlockSpec(memory_space=pltpu.HBM if "out" in far else pltpu.VMEM), out
        ),
        scratch_shapes=list(scratch),
        compiler_params=pltpu.CompilerParams(vmem_limit_bytes=vmem * MIB),
        cost_estimate=pl.CostEstimate(flops=flops, bytes_accessed=moved, transcendentals=0),
    )(*args)


def shape(dims, dtype=bf16):
    return jax.ShapeDtypeStruct(dims, dtype)


def iota(dims, axis):
    return lax.broadcasted_iota(jnp.int32, dims, axis)


def widen():
    row, col = iota((384, 512), 0), iota((384, 512), 1)
    return jnp.where((col % 128 < 96) & (row == col // 128 * 96 + col % 128), 1.0, 0.0).astype(bf16)


def dot(a, b):
    return jnp.dot(a, b, preferred_element_type=f32)


def dot_nt(a, b):
    return lax.dot_general(a, b, (((1,), (1,)), ((), ())), preferred_element_type=f32)


def lanes_of(x):
    return iota(x.shape, 1)


def close(first, middle, last):
    lane = lanes_of(first)
    return (
        jnp.where(lane < 96, first, pltpu.roll(middle, 96, 1)),
        jnp.where(lane < 96, last, pltpu.roll(middle, 64, 1)),
    )


def reopen(first, last, rest):
    lane = lanes_of(first)
    return jnp.where(
        lane < 32, pltpu.roll(first, 32, 1), jnp.where(lane < 64, pltpu.roll(last, 64, 1), rest)
    )


def side_by_side(parts):
    group = lanes_of(parts[0]) // 32
    total = jnp.zeros(parts[0].shape, f32)
    for i, part in enumerate(parts):
        total = jnp.where(group == i, pltpu.roll(part, (32 * i + 64) % 128, 1), total)
    return total


def apart(x, i):
    return pltpu.roll(x, (64 - 32 * i) % 128, 1)


def close_cells(first, middle, last):
    a, b = close(first, middle, last)
    pieces = [middle[8 * g : 8 * g + 8] for g in range(8)]
    return (
        jnp.concatenate([a, side_by_side(pieces[:4])], axis=0),
        jnp.concatenate([b, side_by_side(pieces[4:])], axis=0),
    )


def reopen_cells(first, last):
    rest = [apart(first[64:72], i) for i in range(4)] + [apart(last[64:72], i) for i in range(4)]
    return reopen(first[:64], last[:64], jnp.concatenate(rest, axis=0))


def mode_row(j):
    return pl.ds(j, 128, stride=8)


def close_modes(y_ref, s_ref):
    a, b = close(y_ref[0], y_ref[1], y_ref[2])
    y_ref[0], y_ref[2] = a, b
    y_ref[0, mode_row(6), :] = side_by_side([y_ref[1, mode_row(j), :] for j in range(4)])
    y_ref[2, mode_row(6), :] = side_by_side([y_ref[1, mode_row(j), :] for j in range(4, 6)])
    s_ref[:, 0:128] = y_ref[0].astype(bf16)
    s_ref[:, 128:256] = y_ref[2].astype(bf16)


def reopen_modes(x_ref, y_ref):
    first, last = x_ref[:, 0:128].astype(f32), x_ref[:, 128:256].astype(f32)
    y_ref[0], y_ref[2] = first, last
    y_ref[1] = reopen(first, last, jnp.zeros(first.shape, f32))
    rest = y_ref[0, mode_row(6), :], y_ref[2, mode_row(6), :]
    upper = lanes_of(rest[0]) >= 64
    for j in range(6):
        y_ref[1, mode_row(j), :] = jnp.where(
            upper, apart(rest[j // 4], j % 4), y_ref[1, mode_row(j), :]
        )


def weight_tile(r, og, it):
    index = r * 9 + og * 3 + it
    return index // 7, index % 7


def pack_kernel(x_far, w_far, s_far, x_ref, w_ref, s_ref, in_sems, out_sems):
    arriving = [pltpu.make_async_copy(w_far, w_ref, in_sems.at[4])]
    for a in range(4):
        rows = pl.ds(3 * a, 3)
        arriving.append(pltpu.make_async_copy(x_far.at[rows], x_ref.at[rows], in_sems.at[a]))
    for copy in arriving:
        copy.start()
    arriving[0].wait()
    leaving = []
    spread = widen()
    blank = jnp.zeros((8, 128), f32)
    for a in range(4):
        arriving[a + 1].wait()
        wide = [dot(x_ref[3 * a + t], spread) for t in range(3)]
        for b in range(4):
            first, last = close_cells(*(w[:, b * 128 : (b + 1) * 128] for w in wide))
            tiles = {}
            for r in range(3):
                weights = w_ref[3 * b + r].astype(f32)
                for og in range(3):
                    for it in range(3):
                        tiles[weight_tile(r, og, it)] = weights[
                            8 * og : 8 * og + 8, 128 * it : 128 * it + 128
                        ]
            parts = [tiles.get((a, i), blank) for i in range(7)]
            s_ref[a * 4 + b] = jnp.concatenate([first, last, *parts], axis=0).astype(bf16)
        done = pl.ds(a * 4, 4)
        leaving.append(pltpu.make_async_copy(s_ref.at[done], s_far.at[done], out_sems.at[a]))
        leaving[a].start()
    for copy in leaving:
        copy.wait()


def dft_tables_kernel(p_ref, q_ref, cb_ref, sb_ref, pt_ref, qt_ref, cbt_ref, sbt_ref, c_ref, g_ref):
    for b in range(8):
        c_ref[:, pl.ds(b * 128, 128)] = (
            p_ref[...] * cb_ref[:, b : b + 1] - q_ref[...] * sb_ref[:, b : b + 1]
        ).astype(bf16)
    for b in range(4):
        g_ref[pl.ds(b * 128, 128), :] = (
            pt_ref[...] * cbt_ref[b : b + 1, :] - qt_ref[...] * sbt_ref[b : b + 1, :]
        ).astype(bf16)


def dft_kernel(c_ref, x_ref, w_ref, s_ref, state_ref, part_ref, y_ref):
    for q in range(16):
        cells = x_ref[q].astype(f32)
        first, last = cells[0:72], cells[72:144]
        rows = pl.ds(q * 64, 64)
        state_ref[rows, 0:128] = first[:64].astype(bf16)
        state_ref[rows, 128:256] = reopen_cells(first, last).astype(bf16)
        state_ref[rows, 256:384] = last[:64].astype(bf16)
        part_ref[q] = cells[144:200].astype(bf16)
    for t in range(3):
        for j in (6, 7):
            y_ref[t, mode_row(j), :] = jnp.zeros((128, 128), f32)
    for block in range(3):
        result = dot(c_ref[pl.ds(block * 256, 256), :], state_ref[...]) * w_ref[...]
        for t in range(3):
            for i in range(2):
                y_ref[t, mode_row(2 * block + i), :] = result[
                    i * 128 : (i + 1) * 128, t * 128 : (t + 1) * 128
                ]
    close_modes(y_ref, s_ref)


def legendre_tables_kernel(order_ref, cosine_ref, start_ref, l_ref, rows_ref):
    order = order_ref[...]
    squared = order * order
    rows_ref[...] = jnp.zeros(rows_ref.shape, f32)

    def step(l, carry):
        previous, earlier = carry
        degree = l.astype(f32)
        above = degree > order
        spacing = jnp.where(above, degree * degree - squared, 1.0)
        alpha = jnp.where(
            above, jnp.sqrt(jnp.maximum(4.0 * degree * degree - 1.0, 1.0) / spacing), 0.0
        )
        below = degree - 1.0
        beta = jnp.where(
            degree > order + 1.0,
            jnp.sqrt(
                jnp.maximum(below * below - squared, 0.0)
                / jnp.maximum(4.0 * below * below - 1.0, 1.0)
            ),
            0.0,
        )
        first = degree == order
        current = []
        for t in range(3):
            lanes = pl.ds(t * 128, 128)
            value = alpha * (cosine_ref[:, lanes] * previous[t] - beta * earlier[t]) + jnp.where(
                first, start_ref[:, lanes], 0.0
            )
            rows_ref[t, pl.ds(pl.multiple_of(l * 8, 8), 8), :] = value
            current.append(value)
        return (tuple(current), previous)

    zeros = (jnp.zeros((8, 128), f32),) * 3

    def block(i, carry):
        for u in range(8):
            carry = step(i * 8 + u, carry)
        return carry

    lax.fori_loop(0, 48, block, (zeros, zeros))
    for m3 in range(3):
        for t in range(3):
            parts = [rows_ref[t, pl.ds(r * 8 + m3, 128, stride=24), :] for r in range(3)]
            table = jnp.concatenate(parts, axis=0)
            l_ref[m3, :, pl.ds(t * 128, 128)] = table.astype(bf16)


def legendre_kernel(side, x_ref, l_ref, s_ref, in_ref, out_ref):
    reopen_modes(x_ref, in_ref)
    out_ref[...] = jnp.zeros(out_ref.shape, f32)
    for m3 in range(3):
        halves = [
            jnp.concatenate(
                [in_ref[t, pl.ds(cs * 3 + m3, 128, stride=8), :] for t in range(3)], axis=0
            )
            for cs in range(2)
        ]
        result = lax.dot_general(
            l_ref[m3],
            jnp.concatenate(halves, axis=1).astype(bf16),
            (((side,), (0,)), ((), ())),
            preferred_element_type=f32,
        )
        for t in range(3):
            for cs in range(2):
                out_ref[t, pl.ds(cs * 3 + m3, 128, stride=8), :] = result[
                    t * 128 : (t + 1) * 128, cs * 128 : (cs + 1) * 128
                ]
    close_modes(out_ref, s_ref)


def mix_weight_kernel(place_ref, a_ref, b_ref, c_ref, d_ref, o_ref, full_ref, w_ref):
    for i, ref in enumerate((a_ref, b_ref, c_ref, d_ref)):
        w_ref[(place_ref[0] + 4 - i) % 4] = ref[...].astype(f32)
    spread = widen()
    o_ref[...] = jnp.zeros(o_ref.shape, bf16)
    for r in range(3):
        for og in range(3):
            for it in range(3):
                a, i = weight_tile(r, og, it)
                full_ref[:, og, :, pl.ds(it * 128, 128)] = w_ref[a, :, 8 * i : 8 * i + 8, :]
        part = full_ref[...].reshape(384, 384).astype(bf16)
        wide = dot(part, spread).astype(bf16)
        for b in range(4):
            o_ref[r, pl.ds(b * 128, 96), :] = wide[b * 96 : (b + 1) * 96]


def mix_kernel(x_ref, w_ref, s_ref, in_ref, out_ref):
    reopen_modes(x_ref, in_ref)
    for r in range(3):
        part = in_ref[r].reshape(32, 4, 8, 128)
        modes = jnp.concatenate([part[:, b].reshape(256, 128) for b in range(4)], axis=1)
        mixed = dot_nt(modes.astype(bf16), w_ref[r])
        back = [mixed[:, b * 128 : (b + 1) * 128].reshape(32, 1, 8, 128) for b in range(4)]
        out_ref[r] = jnp.concatenate(back, axis=1).reshape(1024, 128)
    close_modes(out_ref, s_ref)


def inverse_kernel(g_ref, x_ref, state_ref, s_ref, y_ref, m_ref, h_ref):
    reopen_modes(x_ref, y_ref)
    for parity in range(2):
        for j in range(6):
            first = (parity + j % 3) % 2 * 8 + j
            rows = pl.ds(parity * 384 + j * 64, 64)
            for t in range(3):
                part = y_ref[t, pl.ds(first, 64, stride=16), :]
                m_ref[rows, pl.ds(t * 128, 128)] = part.astype(bf16)
    for block in range(2):
        rows = pl.ds(block * 256, 256)
        even = dot(g_ref[rows, 0:384], m_ref[0:384, :])
        odd = dot(g_ref[rows, 384:768], m_ref[384:768, :])
        for half, spatial in enumerate((even + odd, even - odd)):
            rows = pl.ds(half * 512 + block * 256, 256)
            h_ref[rows, :] = state_ref[rows, :].astype(f32) + jax.nn.gelu(spatial)
    row = iota((8, 128), 0)
    for q in range(16):
        inner, halo = [], []
        for t in range(3):
            lanes = pl.ds(t * 128, 128)
            inner.append(h_ref[pl.ds(q * 64, 64), lanes])
            right = h_ref[pl.ds((q + 1) % 16 * 64, 1), lanes]
            left = h_ref[pl.ds((q * 64 + 1023) % 1024, 1), lanes]
            halo.append(jnp.where(row == 0, right, jnp.where(row == 1, left, 0.0)))
        first, last = close_cells(*inner)
        first_halo, last_halo = close(*halo)
        rest = pltpu.roll(halo[1], 64, 1)
        first_halo = jnp.where(row == 2, pltpu.roll(rest, 2, 0), first_halo)
        last_halo = jnp.where(row == 2, pltpu.roll(rest, 1, 0), last_halo)
        s_ref[q, :, 0:128] = jnp.concatenate([first, first_halo], axis=0).astype(bf16)
        s_ref[q, :, 128:256] = jnp.concatenate([last, last_halo], axis=0).astype(bf16)


def with_sides(inner, halo):
    return jnp.concatenate([inner, halo, pltpu.roll(halo, 6, 0)], axis=0).astype(bf16)


def tail_weights_kernel(u_ref, w_ref, o_ref, c_ref, y_ref):
    o_ref[...] = jnp.zeros(o_ref.shape, bf16)
    row, col = iota((1024, 256), 0), iota((1024, 256), 1)
    for q in range(4):
        pick = jnp.where(row == 16 * (col % 64) + 4 * (col // 64) + q, 1.0, 0.0).astype(bf16)
        part = dot(u_ref[...], pick).astype(bf16)
        for b in range(4):
            o_ref[pl.ds(b * 128, 96), pl.ds(q * 256, 256)] = part[b * 96 : (b + 1) * 96]
    for p in range(4):
        blocks = []
        for ds in range(3):
            for window in (0, 1, 2, 3, 4, -1):
                dr = window - p
                if -1 <= dr <= 1:
                    blocks.append(w_ref[3 * (dr + 1) + ds].astype(f32))
                else:
                    blocks.append(jnp.zeros((64, 64), f32))
        wide = jnp.concatenate(blocks, axis=1)
        for t in range(9):
            y_ref[t, pl.ds(p, 64, stride=4), :] = wide[:, t * 128 : (t + 1) * 128]
    for t in range(9):
        c_ref[:, pl.ds(t * 128, 128)] = y_ref[t].astype(bf16)
    row, col = iota((256, 256), 0), iota((256, 256), 1)
    same = (row // 4 == col % 64) & (row % 4 == col // 64)
    c_ref[:, 1152:1408] = jnp.where(same, 1.0, 0.0).astype(bf16)


def fine_kernel(x_ref, u_ref, bias_ref, o_ref, side_ref, h_ref):
    row = iota((8, 128), 0)
    for a in range(4):
        for b in range(4):
            cells = x_ref[a * 4 + b].astype(f32)
            first, last = cells[:, 0:128], cells[:, 128:256]
            first_halo, last_halo = first[72:80], last[72:80]
            rest = jnp.where(
                row == 0,
                pltpu.roll(pltpu.roll(first_halo, 64, 1), 6, 0),
                pltpu.roll(pltpu.roll(last_halo, 64, 1), 7, 0),
            )
            tiles = (
                (first[:64], first_halo),
                (reopen_cells(first, last), reopen(first_halo, last_halo, rest)),
                (last[:64], last_halo),
            )
            for t, (inner, halo) in enumerate(tiles):
                h_ref[pl.ds((a * 3 + t) * 80, 80), pl.ds(b * 128, 128)] = with_sides(inner, halo)
    for q in range(4):
        lanes = pl.ds(q * 256, 256)
        for block in range(4):
            rows = pl.ds(block * 240, 240)
            value = dot(h_ref[rows, :], u_ref[:, lanes]) + bias_ref[:, lanes]
            value = jax.nn.gelu(value).astype(bf16)
            for i in range(3):
                a = block * 3 + i
                o_ref[q, pl.ds(a * 64, 64), :] = value[i * 80 : i * 80 + 64]
                side_ref[q, pl.ds(a * 16, 16), :] = value[i * 80 + 64 : i * 80 + 80]


def conv_kernel(
    ends_ref, f_ref, side_ref, up_ref, down_ref, u_ref, bias_ref, w_ref, cb_ref, o_ref,
    h_ref, e_ref, t_ref, s_ref, z_ref, g_ref,
):
    for b in range(4):
        lanes = pl.ds(b * 128, 128)
        for side, ref in enumerate((up_ref, down_ref)):
            cells = ref[b].astype(f32)
            h_ref[pl.ds(side * 80, 80), lanes] = with_sides(cells[:64], cells[72:80])
    keep = jnp.where(iota((160, 256), 0) < 80, ends_ref[0], ends_ref[1]) > 0

    def around(q, ref, a, size, start):
        half = iota((size, 128), 1) < 64
        below = e_ref[pl.ds(80 + start, size), 0:128]
        above = e_ref[pl.ds(start, size), 128:256]
        if a < 11:
            below = ref[q, pl.ds((a + 1) * size, size), 0:128]
        if a > 0:
            above = ref[q, pl.ds((a - 1) * size, size), 128:256]
        return jnp.where(half, below, above)

    for q in range(4):
        lanes = pl.ds(q * 256, 256)
        value = jax.nn.gelu(dot(h_ref[...], u_ref[:, lanes]) + bias_ref[:, lanes])
        e_ref[...] = jnp.where(keep, value, 0.0).astype(bf16)
        for a in range(12):
            rows = pl.ds(a * 64, 64)
            outer = around(q, f_ref, a, 64, 0)
            t_ref[q, rows, :] = outer
            if q in (0, 3):
                side, amount = (0, 1) if q == 3 else (1, 79)
                edges = pl.ds(a * 16, 16)
                for t in range(3):
                    if t < 2:
                        inner = f_ref[q, rows, t * 128 : (t + 1) * 128]
                        edge = side_ref[q, edges, t * 128 : (t + 1) * 128]
                    else:
                        inner, edge = outer, around(q, side_ref, a, 16, 64)
                    column = jnp.concatenate([inner, edge], axis=0).astype(f32)
                    column = pltpu.roll(column, amount, 0)[:64]
                    s_ref[side, rows, pl.ds(t * 128, 128)] = column.astype(bf16)
    for q in range(4):
        parts = []
        for source in (q - 1, q, q + 1):
            if 0 <= source < 4:
                parts += [f_ref[source], t_ref[source]]
            else:
                parts.append(s_ref[0 if source < 0 else 1])
        total = dot_nt(jnp.concatenate([*parts, f_ref[q]], axis=1), w_ref[...])
        z_ref[q] = (total + cb_ref[...]).astype(bf16)
    row, col = iota((256, 256), 0), iota((256, 256), 1)
    place = jnp.where(col == 4 * (row % 64) + row // 64, 1.0, 0.0).astype(bf16)
    low = iota((32, 8, 256), 1) < 4
    for h in range(6):
        pair = []
        for a in (2 * h, 2 * h + 1):
            cells = jnp.concatenate([z_ref[q, pl.ds(a * 64, 64), :] for q in range(4)], axis=0)
            lines = lax.dot_general(
                cells, place, (((0,), (0,)), ((), ())), preferred_element_type=f32
            )
            pair.append(lines.reshape(32, 8, 256))
        turned = [pltpu.roll(lines, 4, 1) for lines in pair]
        first = jnp.where(low, pair[0], turned[1])
        second = jnp.where(low, turned[0], pair[1])
        both = jnp.stack([first, second], axis=1).reshape(64, 8, 256)
        g_ref[:, pl.ds(8 * h, 8), :] = both
    o_ref[...] = g_ref[...].astype(bf16)


def start_logs(degrees):
    values = []
    total = 0.0
    for m in range(degrees):
        if m > 0:
            total = total + math.log((2.0 * m - 1.0) / (2.0 * m))
        values.append(0.5 * (math.log((2.0 * m + 1.0) / (4.0 * math.pi)) + total))
    return values


def legendre_tables(n):
    order = 3 * n + jnp.arange(8, dtype=jnp.int32)
    lane = jnp.arange(384, dtype=jnp.int32)
    colatitude = ((3 * (lane % 128) + lane // 128).astype(f32) + 0.5) * (math.pi / 384)
    cosine = jnp.broadcast_to(jnp.cos(colatitude)[None, :], (8, 384))
    log_sine = jnp.log(jnp.sin(colatitude))[None, :]
    logs = jnp.asarray(start_logs(384), f32)
    log_base = jnp.sum(jnp.where(order[:, None] == lane[None, :], logs[None, :], 0.0), axis=1)
    log_start = log_base[:, None] + order.astype(f32)[:, None] * log_sine
    start = jnp.where(log_start > -80.0, jnp.exp(jnp.maximum(log_start, -80.0)), 0.0)
    orders = jnp.broadcast_to(order.astype(f32)[:, None], (8, 128))
    return call(
        legendre_tables_kernel,
        shape((3, 384, 384)),
        orders,
        cosine,
        start,
        scratch=[pltpu.VMEM((3, 3072, 128), f32)],
        flops=4 * 10**9,
    )


def dft_tables():
    step = 2.0 * math.pi / 1024

    def waves(wave, sine, y, scale):
        angle = ((wave * y + 256 * sine) % 1024).astype(f32) * step
        return jnp.cos(angle) * scale, jnp.sin(angle) * scale

    def turns(wave, block):
        turn = (wave * block % 8).astype(f32) * (math.pi / 4)
        return jnp.cos(turn), jnp.sin(turn)

    row = jnp.arange(768, dtype=jnp.int32)[:, None]
    wave, sine = 3 * (row % 128) + row // 128 % 3, row // 384
    forward = (*waves(wave, sine, iota((1, 128), 1), 1.0), *turns(wave, iota((1, 8), 1)))
    col = jnp.arange(768, dtype=jnp.int32)[None, :]
    j = col % 384 // 64
    wave = 3 * (2 * (col % 64) + (col // 384 + j % 3) % 2) + j % 3
    scale = jnp.where(wave == 0, 1.0, 2.0)
    inverse = (*waves(wave, j // 3, iota((128, 1), 0), scale), *turns(wave, iota((8, 1), 0)))
    return call(
        dft_tables_kernel,
        (shape((768, 1024)), shape((512, 768))),
        *forward,
        *inverse,
        flops=4 * 10**9,
    )


def exchange(x, axes):
    return lax.all_to_all(x, axes, 0, 0, tiled=True)


def local(state_field, mix_weight, upsample_weight, upsample_bias, conv_weight, conv_bias):
    lat = lax.axis_index("lat")
    n = 4 * lat + lax.axis_index("qa")
    packed = call(
        pack_kernel,
        shape((16, 200, 128)),
        state_field,
        mix_weight,
        far=(0, 1, "out"),
        vmem=60,
        scratch=[
            pltpu.VMEM((12, 64, 384), bf16),
            pltpu.VMEM((12, 24, 384), bf16),
            pltpu.VMEM((16, 200, 128), bf16),
            pltpu.SemaphoreType.DMA((5,)),
            pltpu.SemaphoreType.DMA((4,)),
        ],
        flops=10**9,
    )
    arrived = exchange(packed, ("qa", "qb"))
    forward, inverse = dft_tables()
    basis = legendre_tables(n)
    arrived, basis = lax.optimization_barrier((arrived, basis))
    colatitude = ((3 * n + jnp.arange(384, dtype=jnp.int32) // 128).astype(f32) + 0.5) * (
        math.pi / 384
    )
    scale = (jnp.sin(colatitude) * (math.pi / 384) * (2.0 * math.pi / 1024))[None, :]
    scratch = [pltpu.VMEM((3, 1024, 128), f32)] * 2
    spectra, state, own = call(
        dft_kernel,
        (shape((1024, 256)), shape((1024, 384)), shape((16, 56, 128))),
        forward,
        arrived,
        scale,
        scratch=scratch[:1],
        flops=10**9,
    )
    columns = exchange(spectra, ("lat", "qa"))

    def transform(x, side):
        kernel = functools.partial(legendre_kernel, side)
        return call(kernel, shape((1024, 256)), x, basis, scratch=scratch, flops=10**9)

    coeffs = transform(columns, 1)
    spread_up, spread_conv = call(
        tail_weights_kernel,
        (shape((512, 1024)), shape((256, 1408))),
        upsample_weight,
        conv_weight,
        scratch=[pltpu.VMEM((9, 256, 128), f32)],
        flops=2 * 10**9,
    )
    gathered = [own] + [
        lax.ppermute(own, "qa", [(i, (i + turn) % 4) for i in range(4)]) for turn in (1, 2, 3)
    ]
    degrees = exchange(coeffs, ("lat", "qb"))
    mixer = call(
        mix_weight_kernel,
        shape((3, 512, 512)),
        lax.axis_index("qa").reshape(1).astype(jnp.int32),
        *gathered,
        smem=(0,),
        scratch=[pltpu.VMEM((16, 3, 8, 384), f32), pltpu.VMEM((4, 16, 56, 128), f32)],
        flops=10**9,
    )
    mixed = call(mix_kernel, shape((1024, 256)), degrees, mixer, scratch=scratch, flops=10**9)
    mixed, spread_up, spread_conv = lax.optimization_barrier((mixed, spread_up, spread_conv))
    returned = exchange(mixed, ("lat", "qb"))
    synthesized = transform(returned, 0)
    modes = exchange(synthesized, ("lat", "qa"))
    hidden = call(
        inverse_kernel,
        shape((16, 80, 256)),
        inverse,
        modes,
        state,
        scratch=[scratch[0], pltpu.VMEM((768, 384), bf16), pltpu.VMEM((1024, 384), f32)],
        flops=10**9,
    )
    cells = exchange(hidden, ("qa", "qb"))
    first_row = cells[0:4, :, 0:128]
    last_row = cells[12:16, :, 128:256]
    count = lax.axis_size("lat")
    up = lax.ppermute(last_row, "lat", [(i, i + 1) for i in range(count - 1)])
    down = lax.ppermute(first_row, "lat", [(i + 1, i) for i in range(count - 1)])
    bias = jnp.tile(upsample_bias, 16)[None, :]
    fine, sides = call(
        fine_kernel,
        (shape((4, 768, 256)), shape((4, 192, 256))),
        cells,
        spread_up,
        bias,
        scratch=[pltpu.VMEM((960, 512), bf16)],
        flops=10**10,
    )
    ends = jnp.stack([lat > 0, lat < count - 1]).astype(jnp.int32)
    return call(
        conv_kernel,
        shape((64, 48, 256)),
        ends,
        fine,
        sides,
        up,
        down,
        spread_up,
        bias,
        spread_conv,
        jnp.repeat(conv_bias, 4)[None, :],
        smem=(0,),
        scratch=[
            pltpu.VMEM((160, 512), bf16),
            pltpu.VMEM((160, 256), bf16),
            pltpu.VMEM((4, 768, 128), bf16),
            pltpu.VMEM((2, 768, 384), bf16),
            pltpu.VMEM((4, 768, 256), bf16),
            pltpu.VMEM((64, 48, 256), f32),
        ],
        flops=10**10,
    )


def solution(mesh):
    fine_mesh = Mesh(mesh.devices.reshape(32, 4, 4), ("lat", "qa", "qb"))
    rows = P("lat", ("qa", "qb"), None)
    return jax.shard_map(
        local,
        mesh=fine_mesh,
        in_specs=(rows, rows, P(), P(), P(), P()),
        out_specs=P(None, "lat", ("qa", "qb")),
        check_vma=False,
    )
```
